256 devices in a mesh: dp: 8 (over x, core), cent: 32 (over y, z).
Axes of the slice: x: 4, y: 4, z: 8, core: 2. Of those that a mesh axis runs over, the one named last changes fastest.
Arguments:
- embeddings: bfloat16 [8192, 4096], P('dp', 'cent'), may hold values from -6 to 6
- centroids: bfloat16 [16384, 4096], P('cent'), may hold values from -0.1875 to 0.1875
- assignment: int32 [8192], P('dp'), may hold values from 0 to 16383, as said below
- prior_counts: int32 [16384], P('cent'), may hold values from 1 to 4
Outputs:
- top_score: float32 [8192], P('dp')
- updated: float32 [4096, 16384], P('dp', 'cent')
The draws below stay inside these ranges and needn't reach their ends.
Inputs may be any that keep to these rules, and one draw needn't show every extreme that they name: `assignment`: cluster k belongs to index k // 512 of cent. Among the 1024 rows of one index of dp, at most 64 have clusters that belong to one index of cent, and in every such block of rows some index of cent gets exactly 64 of them.
All inputs are finite; a program needn't handle non-finite values.
Results may differ from the reference program's by a relative error of at most 0.0003.
Values may be sent and summed in bfloat16 or wider, within the bound.
A program may use at most 64 MiB of HBM per device.

```python
import jax
import jax.numpy as jnp
from jax import lax

D = 4096
CENT_DEV = 512
ROWS_DEV = 1024
ROWS = 8192
CENTROIDS = 16384
CAP = 64
N_DP = 8
N_CENT = 32


def draw_assignment(key, part):
    key = jax.random.fold_in(key, 11)

    def one_block(block_key):
        key_full, key_order, key_slots, key_local = jax.random.split(block_key, 4)
        full_owner = jax.random.randint(key_full, (), 0, N_CENT, dtype=jnp.int32)
        order = jax.random.permutation(key_order, ROWS_DEV)
        slots = jax.random.permutation(key_slots, (N_CENT - 1) * CAP)[:ROWS_DEV]
        others = (slots // CAP).astype(jnp.int32)
        others = others + (others >= full_owner).astype(jnp.int32)
        owner = jnp.where(order < CAP, full_owner, others).astype(jnp.int32)
        local = jax.random.randint(key_local, (ROWS_DEV,), 0, CENT_DEV, dtype=jnp.int32)
        return owner * CENT_DEV + local
    block_keys = jax.random.split(key, N_DP)
    return jax.vmap(one_block)(block_keys).reshape(ROWS).astype(jnp.int32)


def touch_ends(values, own_key, low, largest):
    longest = values.shape.index(max(values.shape))
    spots = []
    for shift in (0, 1):
        where = [jax.random.randint(jax.random.fold_in(own_key, axis), (), 0, length) for axis, length in enumerate(values.shape)]
        where[longest] = (where[longest] + shift) % values.shape[longest]
        spots.append(tuple(where))
    return values.at[spots[0]].set(low).at[spots[1]].set(largest)


def level_of(key, dims, cuts, smallest, largest):
    gain, own = 1.0, jax.random.fold_in(key, 6)
    for position, blocks in cuts:
        draws = jnp.exp(jax.random.uniform(jax.random.fold_in(own, position), (blocks,), jnp.float32, smallest / len(cuts), largest / len(cuts)))
        gain = gain * jnp.repeat(draws, dims[position] // blocks).reshape([-1 if axis == position else 1 for axis in range(len(dims))])
    return gain


def bell_draw(rng, extent, width, most, shards=(), held_as=jnp.bfloat16):
    entries = width * jax.random.normal(rng, extent, jnp.float32)
    if shards:
        entries = entries * level_of(rng, extent, shards, -0.22, 0.18)
    return jnp.clip(entries, -most, most).astype(held_as)


def setup_inputs(seed: int = 0) -> dict:
    keys = jax.random.split(jax.random.key(seed), 5)
    return {
        "embeddings": bell_draw(keys[0], (ROWS, D), 1.0, 6.0, ((0, 8), (1, 32))),
        "centroids": bell_draw(keys[1], (CENTROIDS, D), (D // 4) ** -0.5, 0.1875, ((0, 32),)),
        "assignment": draw_assignment(jax.random.fold_in(keys[4], 71), 0),
        "prior_counts": touch_ends(jax.random.randint(keys[3], (CENTROIDS,), 1, 5), jax.random.fold_in(keys[3], 1), 1, 4).astype(jnp.int32),
    }


def reference(embeddings, centroids, assignment, prior_counts):
    cent_f = centroids.astype(jnp.float32)
    half_norm = 0.5 * jnp.sum(cent_f * cent_f, axis=1)
    block = 512
    rows_f = embeddings.astype(jnp.float32).reshape(ROWS // block, block, D) if ROWS % block == 0 else embeddings.astype(jnp.float32).reshape(1, ROWS, D)

    def best_of(rows_block):
        score = jnp.dot(rows_block, cent_f.T, preferred_element_type=jnp.float32) - half_norm[None, :]
        return jnp.max(score, axis=1)

    top_score = lax.map(best_of, rows_f).reshape(ROWS)
    sums = jax.ops.segment_sum(embeddings.astype(jnp.float32), assignment, CENTROIDS)
    counts = jax.ops.segment_sum(jnp.ones((ROWS,), jnp.float32), assignment, CENTROIDS)
    prior = prior_counts.astype(jnp.float32)
    updated = (prior[:, None] * cent_f + sums) / (prior + counts)[:, None]
    return top_score, updated.T
```

```python
import functools

import jax
import jax.numpy as jnp
from jax import lax
from jax.experimental import pallas as pl
from jax.experimental.pallas import tpu as pltpu
from jax.sharding import PartitionSpec as P

NX, NY, NZ = 4, 4, 8
ROWS = 1024
WIDTH = 128
CENT = 512
FEAT = 4096
CAP = 64
SLICE = 512
HEAD = 448
HALF = 256
QUART = CENT // NX
PIECES = 4
PIECE = QUART // PIECES
SLOT_Y = (0, 3, 1, 2)
F32, BF16 = jnp.float32, jnp.bfloat16
NT = (((1,), (1,)), ((), ()))
NN = (((1,), (0,)), ((), ()))


def dot(a, b, dims):
    return lax.dot_general(a, b, dims, preferred_element_type=F32)


def kernel(
    emb, cen, asg, prior, top, num, den,
    e, c, acc, cs, sel, rows, ids_out, ids_in, asg_in, pick, hn, best, best_leaf, best_z, best_y,
    s_za, r_za, s_zb, r_zb, s_ya, r_ya, s_yb, r_yb, s_ext, r_ext, s_la, r_la, s_lb, r_lb,
    s_cc, r_cc, s_x1, r_x1, s_x2, r_x2, s_sel, r_sel, s_ids, r_ids, s_bl, r_bl, s_bz, r_bz, s_by, r_by,
    s_asg, r_asg, l_own, l_c, l_cs,
):
    dp, ce = lax.axis_index("dp"), lax.axis_index("cent")
    x, q, y, z = dp // 2, dp % 2, ce // NZ, ce % NZ
    h = y // 2
    pair = ((y + 1) // 2) % 2
    other_y, across = y + 1 - 2 * (y % 2), 3 - y
    group = 2 * x + h
    is_hub = q == h

    def at(x_, q_, y_, z_):
        return (2 * x_ + q_, NZ * y_ + z_)

    def send(src, dst, ss, rs, dev):
        return pltpu.make_async_remote_copy(
            src_ref=src, dst_ref=dst, send_sem=ss, recv_sem=rs,
            device_id=dev, device_id_type=pl.DeviceIdType.MESH,
        )

    def got(dst, ss, rs):
        send(dst, dst, ss, rs, (dp, ce)).wait_recv()

    def slot(b, k):
        p = pair if b == 0 else 1 - pair
        return 2 * p + (h if k == 0 else 1 - h)

    def zof(d, s):
        return (z + NZ - s) % NZ if d == 0 else (z + s) % NZ

    def za_rows(d, s):
        return pl.ds(0, HEAD) if s < 4 else pl.ds(d * (HEAD // 2), HEAD // 2)

    def zb_rows(d, s):
        n = ROWS - HEAD
        return pl.ds(HEAD, n) if s < 4 else pl.ds(HEAD + d * (n // 2), n // 2)

    def za(d, s, b, k):
        where = e.at[zof(d, s - 1), slot(b, k), za_rows(d, s)]
        src = emb.at[za_rows(d, s)] if (s, b, k) == (1, 0, 0) else where
        return send(src, where, s_za.at[d, s - 1, b, k], r_za.at[d, s - 1, b, k], at(x, q, y, zof(1 - d, 1)))

    def za_got(d, s, b, k):
        got(e.at[zof(d, s), slot(b, k), za_rows(d, s)], s_za.at[d, s - 1, b, k], r_za.at[d, s - 1, b, k])

    def zb(d, s, k):
        where = e.at[zof(d, s - 1), slot(0, k), zb_rows(d, s)]
        src = emb.at[zb_rows(d, s)] if (s, k) == (1, 0) else where
        return send(src, where, s_zb.at[d, s - 1, k], r_zb.at[d, s - 1, k], at(x, q, y, zof(1 - d, 1)))

    def zb_got(d, s, k):
        got(e.at[zof(d, s), slot(0, k), zb_rows(d, s)], s_zb.at[d, s - 1, k], r_zb.at[d, s - 1, k])

    def ya(k):
        where = e.at[z, slot(0, k), pl.ds(0, HEAD)]
        src = emb.at[pl.ds(0, HEAD)] if k == 0 else where
        return send(src, where, s_ya.at[k], r_ya.at[k], at(x, q, other_y, z))

    def ya_got(k):
        got(e.at[z, slot(1, k), pl.ds(0, HEAD)], s_ya.at[k], r_ya.at[k])

    def yb(d, s, k):
        where = e.at[zof(d, s), slot(0, k), zb_rows(d, s)]
        src = emb.at[zb_rows(d, s)] if (s, k) == (0, 0) else where
        return send(src, where, s_yb.at[d, s, k], r_yb.at[d, s, k], at(x, q, other_y, z))

    def yb_got(d, s, k):
        got(e.at[zof(d, s), slot(1, k), zb_rows(d, s)], s_yb.at[d, s, k], r_yb.at[d, s, k])

    def la(d, s):
        where = e.at[zof(d, s), :, pl.ds(0, HEAD)]
        return send(where, where, s_la.at[d, s], r_la.at[d, s], at(x, 1 - q, y, z))

    def lb(d, s):
        where = e.at[zof(d, s), :, pl.ds(HEAD, ROWS - HEAD)]
        return send(where, where, s_lb.at[d, s], r_lb.at[d, s], at(x, 1 - q, y, z))

    def dirs(s):
        return (0,) if s in (0, 4) else (0, 1)

    def sel_send(d, s, k, act, y_to):
        zo = zof(d, s)
        to = at(SLOT_Y[k], zo // 4, y_to, z)
        same = (to[0] == dp) & (to[1] == ce)
        src, dst = sel.at[zo, k], rows.at[group, zo % 4]

        @pl.when(jnp.logical_not(same))
        def _():
            cp = send(src, dst, s_sel.at[d, s, k], r_sel.at[group, zo % 4], to)
            cp.start() if act == "start" else cp.wait_send()

        if act == "start":

            @pl.when(same)
            def _():
                pltpu.make_async_copy(src, dst, r_sel.at[group, zo % 4]).start()

    def ids_send(n, act, y_to):
        to = at(n // 2, n % 2, y_to, z)
        same = (to[0] == dp) & (to[1] == ce)

        @pl.when(jnp.logical_not(same))
        def _():
            cp = send(ids_out, ids_in.at[group], s_ids.at[n], r_ids.at[group], to)
            cp.start() if act == "start" else cp.wait_send()

        if act == "start":

            @pl.when(same)
            def _():
                pltpu.make_async_copy(ids_out, ids_in.at[group], r_ids.at[group]).start()

    def choose(a_ref, y_to):
        a = a_ref[...] - CENT * (NZ * y_to + z)
        mask = (a >= 0) & (a < CENT)
        m = jnp.where(mask, 1.0, 0.0).astype(F32)
        mb = m.astype(BF16)
        i0 = lax.broadcasted_iota(jnp.int32, (128, 128), 0)
        i1 = lax.broadcasted_iota(jnp.int32, (128, 128), 1)
        before = dot(mb, jnp.where(i0 < i1, 1.0, 0.0).astype(BF16), NN)
        total = dot(mb, jnp.ones((128, 128), BF16), NN)
        v = jnp.where(mask, a + 1, 0)
        high, low = (v // 32).astype(F32), (v % 32).astype(F32)
        first = lax.broadcasted_iota(jnp.int32, (8, 128), 0) == 0
        rank_of = lax.broadcasted_iota(jnp.int32, (128, 128), 0).astype(F32)
        off = (CAP * h).astype(F32)
        run = jnp.zeros((1, 128), F32)
        ids = jnp.zeros((8, 128), F32)
        for i in range(8):
            here = m[i : i + 1] > 0.5
            rank = before[i : i + 1] + run
            run = run + total[i : i + 1]
            one = jnp.where((rank == rank_of) & here, 1.0, 0.0).astype(BF16)
            pick[:, 128 * i : 128 * (i + 1)] = one[:CAP]
            put = jnp.where((rank + off == rank_of) & here, 1.0, 0.0).astype(BF16)
            vals = jnp.where(first, high[i : i + 1], low[i : i + 1]).astype(BF16)
            ids = ids + dot(vals, put, NT)
        ids_out[...] = jnp.broadcast_to(32.0 * ids[0:1] + ids[1:2] - 1.0, (8, 128))

    def norms():
        @pl.loop(0, CENT // 128)
        def _(i):
            part = jnp.zeros((128, 128), F32)
            r = pl.ds(pl.multiple_of(i * 128, 128), 128)
            for k in range(FEAT // 128):
                v = c[r, k * 128 : (k + 1) * 128].astype(F32)
                part = part + v * v
            hn[r, :] = 0.5 * jnp.sum(part, axis=1, keepdims=True)

    def work(s, y_to):
        n = len(dirs(s))

        @pl.loop(0, n * (ROWS // HALF))
        def _(t):
            i = t % (ROWS // HALF)
            d = t // (ROWS // HALF)
            zo = (z + NZ - s + 2 * s * d) % NZ
            r = pl.ds(pl.multiple_of(i * HALF, HALF), HALF)
            left = jnp.concatenate(
                [c[:, pl.ds(pl.multiple_of(yy * 1024 + zo * 128, 128), 128)] for yy in SLOT_Y], axis=1
            )
            right = jnp.concatenate([e[zo, k, r, :] for k in range(4)], axis=1)
            got_ = dot(left, right, NT)
            if s == 0:
                acc[i] = got_
            else:
                acc[i] += got_

        for d in dirs(s):
            zo = zof(d, s)
            for k in range(4):
                sel[zo, k] = dot(pick[...], e[zo, k], NN).astype(BF16)
                sel_send(d, s, k, "start", y_to)

    def top_rows():
        for i in range(ROWS // HALF):
            m = jnp.max(acc[i] - hn[...], axis=0, keepdims=True)
            best[2 * i : 2 * i + 1, :] = m[:, :128]
            best[2 * i + 1 : 2 * i + 2, :] = m[:, 128:]

    barrier = pltpu.get_barrier_semaphore()
    peers = [((dp + k) % 8, NZ * yy + z) for k in range(8) for yy in (y, across) if not (k == 0 and yy is y)]
    peers += [(dp, NZ * y + (z + k) % NZ) for k in range(1, NZ)]
    peers += [(dp, NZ * other_y + z), (dp, NZ * (3 - other_y) + z)]
    for to in peers:
        pl.semaphore_signal(barrier, inc=1, device_id=to, device_id_type=pl.DeviceIdType.MESH)
    pl.semaphore_wait(barrier, len(peers))

    own_slice = pltpu.make_async_copy(cen.at[:, pl.ds(pl.multiple_of(dp * SLICE, SLICE), SLICE)], cs, l_cs)

    def tell(act):
        for yy in range(NY):

            @pl.when(yy != y)
            def _():
                cp = send(best_y.at[y % 2], best_y.at[y % 2], s_by.at[yy], r_by.at[y % 2], at(x, q, yy, z))
                cp.start() if act == "start" else cp.wait_send()

    @pl.when(is_hub)
    def _():
        own = pltpu.make_async_copy(emb, e.at[z, slot(0, 0)], l_own)
        all_c = pltpu.make_async_copy(cen, c, l_c)
        give_asg = send(asg, asg_in, s_asg, r_asg, at(x, 1 - q, y, z))
        ya(0).start()
        for d in (0, 1):
            zb(d, 1, 0).start()
        for d in (0, 1):
            za(d, 1, 0, 0).start()
        yb(0, 0, 0).start()
        give_asg.start()
        own.start()
        all_c.start()
        own_slice.start()
        choose(asg, y)
        for n in range(8):
            ids_send(n, "start", y)
        got(e.at[z, slot(0, 1), pl.ds(0, HEAD)], s_ext.at[0], r_ext.at[0])
        ya(1).start()
        for d in (0, 1):
            za(d, 1, 0, 1).start()
        ya_got(0)
        for d in (0, 1):
            za(d, 1, 1, 0).start()
        got(e.at[z, slot(0, 1), pl.ds(HEAD, ROWS - HEAD)], s_ext.at[1], r_ext.at[1])
        for d in (0, 1):
            zb(d, 1, 1).start()
        yb(0, 0, 1).start()
        ya_got(1)
        for d in (0, 1):
            za(d, 1, 1, 1).start()
        own.wait()
        la(0, 0).start()
        all_c.wait()
        norms()
        for s in range(1, 5):
            for k in (0, 1):
                for d in (0, 1):
                    zb_got(d, s, k)
                    if s < 4:
                        zb(d, s + 1, k).start()
                    yb(d, s, k).start()
            for b, k in ((0, 0), (0, 1), (1, 0), (1, 1)):
                for d in (0, 1):
                    za_got(d, s, b, k)
                    if s < 4:
                        za(d, s + 1, b, k).start()
            for d in dirs(s):
                la(d, s).start()
            for d in dirs(s - 1):
                for k in (0, 1):
                    yb_got(d, s - 1, k)
                lb(d, s - 1).start()
            work(s - 1, y)
        for d in (0, 1):
            for k in (0, 1):
                yb_got(d, 4, k)
        lb(0, 4).start()
        work(4, y)
        top_rows()
        got(best_leaf, s_bl, r_bl)
        best_z[z] = jnp.maximum(best[...], best_leaf[...])
        for k in range(1, NZ):
            send(best_z.at[z], best_z.at[z], s_bz.at[k], r_bz.at[k], at(x, q, y, (z + k) % NZ)).start()

    @pl.when(jnp.logical_not(is_hub))
    def _():
        def ext(n):
            r = pl.ds(0, HEAD) if n == 0 else pl.ds(HEAD, ROWS - HEAD)
            return send(emb.at[r], e.at[z, slot(0, 0), r], s_ext.at[n], r_ext.at[n], at(x, q, across, z))

        def part(n, k):
            return pl.ds(pl.multiple_of(((x + n) % NX) * QUART + k * PIECE, PIECE), PIECE)

        def cross(k):
            return send(cen.at[part(0, k)], c.at[part(0, k)], s_cc.at[k], r_cc.at[k], at(x, 1 - q, across, z))

        def near(d, k):
            to = at((x + 1 + 2 * d) % NX, q, y, z)
            return send(c.at[part(0, k)], c.at[part(0, k)], s_x1.at[d, k], r_x1.at[d, k], to)

        def far(k):
            d = k // 2
            to = at((x + 1 + 2 * d) % NX, q, y, z)
            which = part(3 - 2 * d, k)
            return send(c.at[which], c.at[which], s_x2.at[k], r_x2.at[k], to)

        ext(0).start()
        ext(1).start()
        own_slice.start()
        for n in (0, 1):
            ext(n).wait_send()
        for k in range(PIECES):
            cross(k).start()
        got(asg_in, s_asg, r_asg)
        choose(asg_in, across)
        for n in range(8):
            ids_send(n, "start", across)
        for k in range(PIECES):
            got(c.at[part(0, k)], s_cc.at[k], r_cc.at[k])
            for d in (0, 1):
                near(d, k).start()
            if k:
                for d in (0, 1):
                    got(c.at[part(3 - 2 * d, k - 1)], s_x1.at[d, k - 1], r_x1.at[d, k - 1])
                far(k - 1).start()
        for d in (0, 1):
            got(c.at[part(3 - 2 * d, PIECES - 1)], s_x1.at[d, PIECES - 1], r_x1.at[d, PIECES - 1])
        far(PIECES - 1).start()
        for k in range(PIECES):
            got(c.at[part(2, k)], s_x2.at[k], r_x2.at[k])
        norms()
        for s in range(5):
            for d in dirs(s):
                got(e.at[zof(d, s), :, pl.ds(0, HEAD)], s_la.at[d, s], r_la.at[d, s])
                got(e.at[zof(d, s), :, pl.ds(HEAD, ROWS - HEAD)], s_lb.at[d, s], r_lb.at[d, s])
            work(s, across)
        top_rows()
        give = send(best, best_leaf, s_bl, r_bl, at(x, 1 - q, y, z))
        give.start()
        for n in (0, 1):
            pass
        for k in range(PIECES):
            cross(k).wait_send()
            far(k).wait_send()
            for d in (0, 1):
                near(d, k).wait_send()
        for n in range(8):
            ids_send(n, "wait", across)
        for s in range(5):
            for d in dirs(s):
                for k in range(4):
                    sel_send(d, s, k, "wait", across)
        give.wait_send()

    own_slice.wait()
    pr = prior[...].astype(F32)
    for n in range(8):
        got(ids_in.at[n], s_ids.at[n], r_ids.at[n])
    k_of = lax.broadcasted_iota(jnp.int32, (CENT, 128), 0).astype(F32)
    hot = jnp.concatenate(
        [
            jnp.where(jnp.maximum(ids_in[2 * n, 0:1], ids_in[2 * n + 1, 0:1]) == k_of, 1.0, 0.0).astype(BF16)
            for n in range(4)
        ],
        axis=1,
    )
    counts = dot(jnp.ones((8, SLICE), BF16), hot, NT)
    den[...] = jnp.broadcast_to(pr + counts[0:1], (8, CENT))
    for n in range(8):
        for k in range(4):
            got(rows.at[n, k], s_sel.at[0, 0, 0], r_sel.at[n, k])
    for k in range(4):
        f = slice(k * 128, (k + 1) * 128)
        taken = jnp.concatenate([rows[n, k] for n in range(8)], axis=0)
        num[f, :] = pr * cs[:, f].astype(F32).T + dot(taken.T, hot, NT)

    @pl.when(is_hub)
    def _():
        for k in range(1, NZ):
            zs = (z + NZ - k) % NZ
            got(best_z.at[zs], s_bz.at[k], r_bz.at[k])
        m = best_z[0]
        for k in range(1, NZ):
            m = jnp.maximum(m, best_z[k])
        best_y[y % 2] = m
        tell("start")
        got(best_y.at[1 - y % 2], s_by.at[0], r_by.at[1 - y % 2])
        for s in range(1, 5):
            for d in (0, 1):
                for k in (0, 1):
                    zb(d, s, k).wait_send()
                    yb(d, s, k).wait_send()
                    for b in (0, 1):
                        za(d, s, b, k).wait_send()
        for k in (0, 1):
            ya(k).wait_send()
            yb(0, 0, k).wait_send()
        for s in range(5):
            for d in dirs(s):
                la(d, s).wait_send()
                lb(d, s).wait_send()
                for k in range(4):
                    sel_send(d, s, k, "wait", y)
        for n in range(8):
            ids_send(n, "wait", y)
        send(asg, asg_in, s_asg, r_asg, at(x, 1 - q, y, z)).wait_send()
        for k in range(1, NZ):
            send(best_z.at[z], best_z.at[z], s_bz.at[k], r_bz.at[k], at(x, q, y, (z + k) % NZ)).wait_send()
        tell("wait")

    @pl.when(jnp.logical_not(is_hub))
    def _():
        for n in (0, 1):
            got(best_y.at[n], s_by.at[n], r_by.at[n])

    top[...] = jnp.maximum(best_y[0], best_y[1])


def on_device(embeddings, centroids, assignment, prior_counts):
    dma = pltpu.SemaphoreType.DMA
    both = lambda *shape: [dma(shape), dma(shape)]
    vmem, hbm = pl.BlockSpec(memory_space=pltpu.VMEM), pl.BlockSpec(memory_space=pl.ANY)
    top, num, den = pl.pallas_call(
        kernel,
        out_shape=[
            jax.ShapeDtypeStruct((8, 128), F32),
            jax.ShapeDtypeStruct((SLICE, CENT), F32),
            jax.ShapeDtypeStruct((8, CENT), F32),
        ],
        in_specs=[hbm, hbm, vmem, vmem],
        out_specs=[vmem, vmem, vmem],
        scratch_shapes=[
            pltpu.VMEM((NZ, 4, ROWS, WIDTH), BF16),
            pltpu.VMEM((CENT, FEAT), BF16),
            pltpu.VMEM((ROWS // HALF, CENT, HALF), F32),
            pltpu.VMEM((CENT, SLICE), BF16),
            pltpu.VMEM((NZ, 4, CAP, WIDTH), BF16),
            pltpu.VMEM((8, 4, CAP, WIDTH), BF16),
            pltpu.VMEM((8, 128), F32),
            pltpu.VMEM((8, 8, 128), F32),
            pltpu.VMEM((8, 128), jnp.int32),
            pltpu.VMEM((CAP, ROWS), BF16),
            pltpu.VMEM((CENT, 1), F32),
            pltpu.VMEM((8, 128), F32),
            pltpu.VMEM((8, 128), F32),
            pltpu.VMEM((NZ, 8, 128), F32),
            pltpu.VMEM((2, 8, 128), F32),
            *both(2, 4, 2, 2),
            *both(2, 4, 2),
            *both(2),
            *both(2, 5, 2),
            *both(2),
            *both(2, 5),
            *both(2, 5),
            *both(PIECES),
            *both(2, PIECES),
            *both(PIECES),
            dma((2, 5, 4)), dma((8, 4)),
            *both(8),
            dma(()), dma(()),
            *both(NZ),
            dma((4,)), dma((2,)),
            dma(()), dma(()),
            dma(()), dma(()), dma(()),
        ],
        compiler_params=pltpu.CompilerParams(
            collective_id=0, has_side_effects=True, vmem_limit_bytes=40 * 2**20
        ),
        name="score_and_update",
    )(embeddings, centroids, assignment.reshape(8, 128), prior_counts.reshape(1, CENT))
    return top.reshape(ROWS), num / den[0:1]


def solution(mesh):
    placed = (P("dp", "cent"), P("cent", None), P("dp"), P("cent"))
    return jax.shard_map(
        on_device, mesh=mesh, in_specs=placed, out_specs=(P("dp"), P("dp", "cent")), check_vma=False
    )
```

```python
import functools

import jax
import jax.numpy as jnp
from jax import lax
from jax.experimental import pallas as pl
from jax.experimental.pallas import tpu as pltpu
from jax.sharding import PartitionSpec as P

NX, NY, NZ = 4, 4, 8
ROWS = 1024
WIDTH = 128
CENT = 512
FEAT = 4096
CAP = 64
SLICE = 512
HEAD = 448
QUART = CENT // NX
PIECES = 8
PIECE = QUART // PIECES
SLOT_Y = (0, 3, 1, 2)
F32, BF16 = jnp.float32, jnp.bfloat16
NT = (((1,), (1,)), ((), ()))
NN = (((1,), (0,)), ((), ()))


def dot(a, b, dims):
    return lax.dot_general(a, b, dims, preferred_element_type=F32)


def kernel(
    emb, cen, asg_hbm, prior_hbm, top, num, den,
    e, c, acc, cs, sel, rows, ids_out, ids_in, asg, asg_in, prior, pick, hn, best, best_leaf, best_z, best_y,
    s_za, r_za, s_zb, r_zb, s_ya, r_ya, s_yb, r_yb, s_ext, r_ext, s_la, r_la, s_lb, r_lb,
    s_cc, r_cc, s_x1, r_x1, s_x2, r_x2, s_sel, r_sel, s_ids, r_ids, s_bl, r_bl, s_bz, r_bz, s_by, r_by,
    s_asg, r_asg, l_own, l_c, l_cs, l_asg, l_prior,
):
    dp, ce = lax.axis_index("dp"), lax.axis_index("cent")
    x, q, y, z = dp // 2, dp % 2, ce // NZ, ce % NZ
    h = y // 2
    pair = ((y + 1) // 2) % 2
    other_y, across = y + 1 - 2 * (y % 2), 3 - y
    group = 2 * x + h
    is_hub = q == h

    def at(x_, q_, y_, z_):
        return (2 * x_ + q_, NZ * y_ + z_)

    def send(src, dst, ss, rs, dev):
        return pltpu.make_async_remote_copy(
            src_ref=src, dst_ref=dst, send_sem=ss, recv_sem=rs,
            device_id=dev, device_id_type=pl.DeviceIdType.MESH,
        )

    def got(dst, ss, rs):
        send(dst, dst, ss, rs, (dp, ce)).wait_recv()

    def slot(b, k):
        p = pair if b == 0 else 1 - pair
        return 2 * p + (h if k == 0 else 1 - h)

    def zof(d, s):
        return (z + NZ - s) % NZ if d == 0 else (z + s) % NZ

    def za_rows(d, s):
        return pl.ds(0, HEAD) if s < 4 else pl.ds(d * (HEAD // 2), HEAD // 2)

    def zb_rows(d, s):
        n = ROWS - HEAD
        return pl.ds(HEAD, n) if s < 4 else pl.ds(HEAD + d * (n // 2), n // 2)

    def za(d, s, b, k):
        where = e.at[zof(d, s - 1), slot(b, k), za_rows(d, s)]
        src = emb.at[za_rows(d, s)] if (s, b, k) == (1, 0, 0) else where
        return send(src, where, s_za.at[d, s - 1, b, k], r_za.at[d, s - 1, b, k], at(x, q, y, zof(1 - d, 1)))

    def za_got(d, s, b, k):
        got(e.at[zof(d, s), slot(b, k), za_rows(d, s)], s_za.at[d, s - 1, b, k], r_za.at[d, s - 1, b, k])

    def zb(d, s, k):
        where = e.at[zof(d, s - 1), slot(0, k), zb_rows(d, s)]
        src = emb.at[zb_rows(d, s)] if (s, k) == (1, 0) else where
        return send(src, where, s_zb.at[d, s - 1, k], r_zb.at[d, s - 1, k], at(x, q, y, zof(1 - d, 1)))

    def zb_got(d, s, k):
        got(e.at[zof(d, s), slot(0, k), zb_rows(d, s)], s_zb.at[d, s - 1, k], r_zb.at[d, s - 1, k])

    def ya(k):
        where = e.at[z, slot(0, k), pl.ds(0, HEAD)]
        src = emb.at[pl.ds(0, HEAD)] if k == 0 else where
        return send(src, where, s_ya.at[k], r_ya.at[k], at(x, q, other_y, z))

    def ya_got(k):
        got(e.at[z, slot(1, k), pl.ds(0, HEAD)], s_ya.at[k], r_ya.at[k])

    def yb(d, s, k):
        where = e.at[zof(d, s), slot(0, k), zb_rows(d, s)]
        src = emb.at[zb_rows(d, s)] if (s, k) == (0, 0) else where
        return send(src, where, s_yb.at[d, s, k], r_yb.at[d, s, k], at(x, q, other_y, z))

    def yb_got(d, s, k):
        got(e.at[zof(d, s), slot(1, k), zb_rows(d, s)], s_yb.at[d, s, k], r_yb.at[d, s, k])

    def la(d, s):
        where = e.at[zof(d, s), :, pl.ds(0, HEAD)]
        return send(where, where, s_la.at[d, s], r_la.at[d, s], at(x, 1 - q, y, z))

    def lb(d, s):
        where = e.at[zof(d, s), :, pl.ds(HEAD, ROWS - HEAD)]
        return send(where, where, s_lb.at[d, s], r_lb.at[d, s], at(x, 1 - q, y, z))

    def dirs(s):
        return (0,) if s in (0, 4) else (0, 1)

    def blocks(s):
        return (0, 1) if s == 0 else (2 * s - 1, min(2 * s + 1, NZ))

    def zon(n):
        far = (n + 1) // 2
        return (z + NZ + far * (1 - 2 * (n % 2))) % NZ

    def sel_send(n, k, act, y_to):
        zo = zon(n)
        to = at(SLOT_Y[k], zo // 4, y_to, z)
        same = (to[0] == dp) & (to[1] == ce)
        src, dst = sel.at[zo, k], rows.at[group, zo % 4]

        @pl.when(jnp.logical_not(same))
        def _():
            cp = send(src, dst, s_sel.at[n, k], r_sel.at[group, zo % 4], to)
            cp.start() if act == "start" else cp.wait_send()

        if act == "start":

            @pl.when(same)
            def _():
                pltpu.make_async_copy(src, dst, r_sel.at[group, zo % 4]).start()

    def ids_send(n, act, y_to):
        to = at(n // 2, n % 2, y_to, z)
        same = (to[0] == dp) & (to[1] == ce)

        @pl.when(jnp.logical_not(same))
        def _():
            cp = send(ids_out, ids_in.at[group], s_ids.at[n], r_ids.at[group], to)
            cp.start() if act == "start" else cp.wait_send()

        if act == "start":

            @pl.when(same)
            def _():
                pltpu.make_async_copy(ids_out, ids_in.at[group], r_ids.at[group]).start()

    def choose(a_ref, y_to):
        a = a_ref[...] - CENT * (NZ * y_to + z)
        mask = (a >= 0) & (a < CENT)
        m = jnp.where(mask, 1.0, 0.0).astype(F32)
        mb = m.astype(BF16)
        i0 = lax.broadcasted_iota(jnp.int32, (128, 128), 0)
        i1 = lax.broadcasted_iota(jnp.int32, (128, 128), 1)
        before = dot(mb, jnp.where(i0 < i1, 1.0, 0.0).astype(BF16), NN)
        total = dot(mb, jnp.ones((128, 128), BF16), NN)
        v = jnp.where(mask, a + 1, 0)
        high, low = (v // 32).astype(F32), (v % 32).astype(F32)
        first = lax.broadcasted_iota(jnp.int32, (8, 128), 0) == 0
        rank_of = lax.broadcasted_iota(jnp.int32, (128, 128), 0).astype(F32)
        off = (CAP * h).astype(F32)
        run = jnp.zeros((1, 128), F32)
        ids = jnp.zeros((8, 128), F32)
        for i in range(8):
            here = m[i : i + 1] > 0.5
            rank = before[i : i + 1] + run
            run = run + total[i : i + 1]
            one = jnp.where((rank == rank_of) & here, 1.0, 0.0).astype(BF16)
            pick[:, 128 * i : 128 * (i + 1)] = one[:CAP]
            put = jnp.where((rank + off == rank_of) & here, 1.0, 0.0).astype(BF16)
            vals = jnp.where(first, high[i : i + 1], low[i : i + 1]).astype(BF16)
            ids = ids + dot(vals, put, NT)
        ids_out[...] = jnp.broadcast_to(32.0 * ids[0:1] + ids[1:2] - 1.0, (8, 128))

    def norms(first, count):
        @pl.loop(0, count)
        def _(i):
            part = jnp.zeros((128, 128), F32)
            r = pl.ds(pl.multiple_of((first + i) % NX * 128, 128), 128)
            for k in range(FEAT // 128):
                v = c[r, k * 128 : (k + 1) * 128].astype(F32)
                part = part + v * v
            hn[r, :] = 0.5 * jnp.sum(part, axis=1, keepdims=True)

    def choose_rows(lo, hi, y_to):
        @pl.loop(lo, hi)
        def _(n):
            zo = zon(n)
            for k in range(4):
                sel[zo, k] = dot(pick[...], e[zo, k], NN).astype(BF16)
                sel_send(n, k, "start", y_to)

    def score(lo, hi):
        def one(n):
            zo = zon(n)
            left = jnp.concatenate(
                [c[:, pl.ds(pl.multiple_of(yy * 1024 + zo * 128, 128), 128)] for yy in SLOT_Y], axis=1
            )
            return dot(left, jnp.concatenate([e[zo, k] for k in range(4)], axis=1), NT)

        if lo == 0:
            acc[...] = one(0)
        else:

            @pl.loop(lo, hi)
            def _(n):
                acc[...] += one(n)

    def top_rows():
        m = jnp.max(acc[...] - hn[...], axis=0, keepdims=True)
        for i in range(8):
            best[i : i + 1, :] = m[:, 128 * i : 128 * (i + 1)]

    barrier = pltpu.get_barrier_semaphore()
    own_slice = pltpu.make_async_copy(cen.at[:, pl.ds(pl.multiple_of(dp * SLICE, SLICE), SLICE)], cs, l_cs)
    own_asg = pltpu.make_async_copy(asg_hbm, asg, l_asg)
    own_prior = pltpu.make_async_copy(prior_hbm, prior, l_prior)
    own_asg.start()
    own_prior.start()
    own_slice.start()
    peers = [((dp + k) % 8, NZ * yy + z) for k in range(8) for yy in (y, across) if not (k == 0 and yy is y)]
    peers += [(dp, NZ * y + (z + k) % NZ) for k in range(1, NZ)]
    peers += [(dp, NZ * other_y + z), (dp, NZ * (3 - other_y) + z)]
    for to in peers:
        pl.semaphore_signal(barrier, inc=1, device_id=to, device_id_type=pl.DeviceIdType.MESH)
    pl.semaphore_wait(barrier, len(peers))

    def tell(act):
        for yy in range(NY):

            @pl.when(yy != y)
            def _():
                cp = send(best_y.at[y % 2], best_y.at[y % 2], s_by.at[yy], r_by.at[y % 2], at(x, q, yy, z))
                cp.start() if act == "start" else cp.wait_send()

    @pl.when(is_hub)
    def _():
        own = pltpu.make_async_copy(emb, e.at[z, slot(0, 0)], l_own)
        all_c = pltpu.make_async_copy(cen, c, l_c)
        give_asg = send(asg, asg_in, s_asg, r_asg, at(x, 1 - q, y, z))
        for d in (0, 1):
            zb(d, 1, 0).start()
        for d in (0, 1):
            za(d, 1, 0, 0).start()
        ya(0).start()
        yb(0, 0, 0).start()
        own.start()
        all_c.start()
        own_asg.wait()
        give_asg.start()
        got(e.at[z, slot(0, 1), pl.ds(0, HEAD)], s_ext.at[0], r_ext.at[0])
        ya(1).start()
        for d in (0, 1):
            za(d, 1, 0, 1).start()
        ya_got(0)
        for d in (0, 1):
            za(d, 1, 1, 0).start()
        got(e.at[z, slot(0, 1), pl.ds(HEAD, ROWS - HEAD)], s_ext.at[1], r_ext.at[1])
        for d in (0, 1):
            zb(d, 1, 1).start()
        yb(0, 0, 1).start()
        ya_got(1)
        for d in (0, 1):
            za(d, 1, 1, 1).start()
        own.wait()
        la(0, 0).start()
        for s in range(1, 5):
            for k in (0, 1):
                for d in (0, 1):
                    zb_got(d, s, k)
                    if s < 4:
                        zb(d, s + 1, k).start()
                    yb(d, s, k).start()
            if s == 1:
                choose(asg, y)
                for n in range(8):
                    ids_send(n, "start", y)
            for b, k in ((0, 0), (0, 1), (1, 0), (1, 1)):
                for d in (0, 1):
                    za_got(d, s, b, k)
                    if s < 4:
                        za(d, s + 1, b, k).start()
            for d in dirs(s):
                la(d, s).start()
            for d in dirs(s - 1):
                for k in (0, 1):
                    yb_got(d, s - 1, k)
                lb(d, s - 1).start()
            if s == 1:
                all_c.wait()
                norms(0, NX)
            choose_rows(*blocks(s - 1), y)
            score(*blocks(s - 1))
        for d in (0, 1):
            for k in (0, 1):
                yb_got(d, 4, k)
        lb(0, 4).start()
        choose_rows(*blocks(4), y)
        score(*blocks(4))
        top_rows()
        got(best_leaf, s_bl, r_bl)
        best_z[z] = jnp.maximum(best[...], best_leaf[...])
        for k in range(1, NZ):
            send(best_z.at[z], best_z.at[z], s_bz.at[k], r_bz.at[k], at(x, q, y, (z + k) % NZ)).start()

    @pl.when(jnp.logical_not(is_hub))
    def _():
        def ext(n):
            r = pl.ds(0, HEAD) if n == 0 else pl.ds(HEAD, ROWS - HEAD)
            return send(emb.at[r], e.at[z, slot(0, 0), r], s_ext.at[n], r_ext.at[n], at(x, q, across, z))

        def part(n, k):
            return pl.ds(pl.multiple_of(((x + n) % NX) * QUART + k * PIECE, PIECE), PIECE)

        def cross(k):
            return send(cen.at[part(0, k)], c.at[part(0, k)], s_cc.at[k], r_cc.at[k], at(x, 1 - q, across, z))

        def near(d, k):
            to = at((x + 1 + 2 * d) % NX, q, y, z)
            return send(c.at[part(0, k)], c.at[part(0, k)], s_x1.at[d, k], r_x1.at[d, k], to)

        def far(k):
            d = k // (PIECES // 2)
            to = at((x + 1 + 2 * d) % NX, q, y, z)
            which = part(3 - 2 * d, k)
            return send(c.at[which], c.at[which], s_x2.at[k], r_x2.at[k], to)

        ext(0).start()
        ext(1).start()
        own_asg.wait()
        for n in (0, 1):
            ext(n).wait_send()
        for k in range(PIECES):
            cross(k).start()
        got(asg_in, s_asg, r_asg)
        choose(asg_in, across)
        for n in range(8):
            ids_send(n, "start", across)

        def pass_on(k):
            for d in (0, 1):
                got(c.at[part(3 - 2 * d, k)], s_x1.at[d, k], r_x1.at[d, k])
            far(k).start()

        def arrived(s):
            for d in dirs(s):
                got(e.at[zof(d, s), :, pl.ds(0, HEAD)], s_la.at[d, s], r_la.at[d, s])
                got(e.at[zof(d, s), :, pl.ds(HEAD, ROWS - HEAD)], s_lb.at[d, s], r_lb.at[d, s])
            choose_rows(*blocks(s), across)

        for k in range(PIECES):
            got(c.at[part(0, k)], s_cc.at[k], r_cc.at[k])
            for d in (0, 1):
                near(d, k).start()
            if k > 1:
                pass_on(k - 2)
        arrived(0)
        for k in range(PIECES - 2, PIECES):
            pass_on(k)
        norms(x, 2)
        norms(x + 3, 1)
        arrived(1)
        arrived(2)
        for k in range(PIECES):
            got(c.at[part(2, k)], s_x2.at[k], r_x2.at[k])
        norms(x + 2, 1)
        score(0, 1)
        score(1, 5)
        for s in (3, 4):
            arrived(s)
            score(*blocks(s))
        top_rows()
        give = send(best, best_leaf, s_bl, r_bl, at(x, 1 - q, y, z))
        give.start()
        for k in range(PIECES):
            cross(k).wait_send()
            far(k).wait_send()
            for d in (0, 1):
                near(d, k).wait_send()
        for n in range(8):
            ids_send(n, "wait", across)
        for n in range(NZ):
            for k in range(4):
                sel_send(n, k, "wait", across)
        give.wait_send()

    own_slice.wait()
    own_prior.wait()
    pr = prior[...].astype(F32)
    for n in range(8):
        got(ids_in.at[n], s_ids.at[n], r_ids.at[n])
    k_of = lax.broadcasted_iota(jnp.int32, (CENT, 128), 0).astype(F32)
    hot = jnp.concatenate(
        [
            jnp.where(jnp.maximum(ids_in[2 * n, 0:1], ids_in[2 * n + 1, 0:1]) == k_of, 1.0, 0.0).astype(BF16)
            for n in range(4)
        ],
        axis=1,
    )
    counts = dot(jnp.ones((8, SLICE), BF16), hot, NT)
    den[...] = pr + counts[0:1]
    for n in range(8):
        for k in range(4):
            got(rows.at[n, k], s_sel.at[0, 0], r_sel.at[n, k])
    for k in range(4):
        f = slice(k * 128, (k + 1) * 128)
        taken = jnp.concatenate([rows[n, k] for n in range(8)], axis=0)
        num[f, :] = pr * cs[:, f].astype(F32).T + dot(taken.T, hot, NT)

    @pl.when(is_hub)
    def _():
        for k in range(1, NZ):
            zs = (z + NZ - k) % NZ
            got(best_z.at[zs], s_bz.at[k], r_bz.at[k])
        m = best_z[0]
        for k in range(1, NZ):
            m = jnp.maximum(m, best_z[k])
        best_y[y % 2] = m
        tell("start")
        got(best_y.at[1 - y % 2], s_by.at[0], r_by.at[1 - y % 2])
        for s in range(1, 5):
            for d in (0, 1):
                for k in (0, 1):
                    zb(d, s, k).wait_send()
                    yb(d, s, k).wait_send()
                    for b in (0, 1):
                        za(d, s, b, k).wait_send()
        for k in (0, 1):
            ya(k).wait_send()
            yb(0, 0, k).wait_send()
        for s in range(5):
            for d in dirs(s):
                la(d, s).wait_send()
                lb(d, s).wait_send()
        for n in range(NZ):
            for k in range(4):
                sel_send(n, k, "wait", y)
        for n in range(8):
            ids_send(n, "wait", y)
        send(asg, asg_in, s_asg, r_asg, at(x, 1 - q, y, z)).wait_send()
        for k in range(1, NZ):
            send(best_z.at[z], best_z.at[z], s_bz.at[k], r_bz.at[k], at(x, q, y, (z + k) % NZ)).wait_send()
        tell("wait")

    @pl.when(jnp.logical_not(is_hub))
    def _():
        for n in (0, 1):
            got(best_y.at[n], s_by.at[n], r_by.at[n])

    top[...] = jnp.maximum(best_y[0], best_y[1])


def on_device(embeddings, centroids, assignment, prior_counts):
    dma = pltpu.SemaphoreType.DMA
    both = lambda *shape: [dma(shape), dma(shape)]
    vmem, hbm = pl.BlockSpec(memory_space=pltpu.VMEM), pl.BlockSpec(memory_space=pltpu.HBM)
    placed = (embeddings, centroids, assignment.reshape(8, 128), prior_counts.reshape(1, CENT))
    placed = [pltpu.with_memory_space_constraint(v, pltpu.HBM) for v in placed]
    top, num, den = pl.pallas_call(
        kernel,
        out_shape=[
            jax.ShapeDtypeStruct((8, 128), F32),
            jax.ShapeDtypeStruct((SLICE, CENT), F32),
            jax.ShapeDtypeStruct((1, CENT), F32),
        ],
        in_specs=[hbm, hbm, hbm, hbm],
        out_specs=[vmem, vmem, vmem],
        scratch_shapes=[
            pltpu.VMEM((NZ, 4, ROWS, WIDTH), BF16),
            pltpu.VMEM((CENT, FEAT), BF16),
            pltpu.VMEM((CENT, ROWS), F32),
            pltpu.VMEM((CENT, SLICE), BF16),
            pltpu.VMEM((NZ, 4, CAP, WIDTH), BF16),
            pltpu.VMEM((8, 4, CAP, WIDTH), BF16),
            pltpu.VMEM((8, 128), F32),
            pltpu.VMEM((8, 8, 128), F32),
            pltpu.VMEM((8, 128), jnp.int32),
            pltpu.VMEM((8, 128), jnp.int32),
            pltpu.VMEM((1, CENT), jnp.int32),
            pltpu.VMEM((CAP, ROWS), BF16),
            pltpu.VMEM((CENT, 1), F32),
            pltpu.VMEM((8, 128), F32),
            pltpu.VMEM((8, 128), F32),
            pltpu.VMEM((NZ, 8, 128), F32),
            pltpu.VMEM((2, 8, 128), F32),
            *both(2, 4, 2, 2),
            *both(2, 4, 2),
            *both(2),
            *both(2, 5, 2),
            *both(2),
            *both(2, 5),
            *both(2, 5),
            *both(PIECES),
            *both(2, PIECES),
            *both(PIECES),
            dma((NZ, 4)), dma((8, 4)),
            *both(8),
            dma(()), dma(()),
            *both(NZ),
            dma((4,)), dma((2,)),
            dma(()), dma(()),
            *both(), *both(), dma(()),
        ],
        compiler_params=pltpu.CompilerParams(
            collective_id=0, has_side_effects=True, vmem_limit_bytes=40 * 2**20
        ),
        name="score_and_update",
    )(*placed)
    return top.reshape(ROWS), num / den


def solution(mesh):
    placed = (P("dp", "cent"), P("cent", None), P("dp"), P("cent"))
    return jax.shard_map(
        on_device, mesh=mesh, in_specs=placed, out_specs=(P("dp"), P("dp", "cent")), check_vma=False
    )
```

```python
import functools

import jax
import jax.numpy as jnp
from jax import lax
from jax.experimental import pallas as pl
from jax.experimental.pallas import tpu as pltpu
from jax.sharding import PartitionSpec as P

NX, NY, NZ = 4, 4, 8
ROWS = 1024
WIDTH = 128
CENT = 512
FEAT = 4096
CAP = 64
SLICE = 512
HEAD = 448
QUART = CENT // NX
PIECES = 8
PIECE = QUART // PIECES
SLOT_Y = (0, 3, 1, 2)
F32, BF16 = jnp.float32, jnp.bfloat16
NT = (((1,), (1,)), ((), ()))
NN = (((1,), (0,)), ((), ()))


def dot(a, b, dims):
    return lax.dot_general(a, b, dims, preferred_element_type=F32)


def kernel(
    emb, cen, asg_hbm, prior_hbm, top, num, den,
    e, c, acc, cs, sel, rows, ids_out, ids_in, asg, asg_in, prior, pick, hn, best, best_leaf, best_z, best_y,
    s_ring, r_za, r_zb, r_ya, r_yb, s_ext, r_ext, s_l, r_la, r_lb, r_l4,
    s_c, r_cc, r_x1, r_x2, s_sel, r_sel, s_ids, r_ids, s_bl, r_bl, s_bz, r_bz, s_by, r_by,
    s_asg, r_asg, l_own, l_c, l_cs, l_asg, l_prior,
):
    dp, ce = lax.axis_index("dp"), lax.axis_index("cent")
    x, q, y, z = dp // 2, dp % 2, ce // NZ, ce % NZ
    h = y // 2
    pair = ((y + 1) // 2) % 2
    other_y, across = y + 1 - 2 * (y % 2), 3 - y
    group = 2 * x + h
    is_hub = q == h

    def at(x_, q_, y_, z_):
        return (2 * x_ + q_, NZ * y_ + z_)

    def send(src, dst, ss, rs, dev):
        return pltpu.make_async_remote_copy(
            src_ref=src, dst_ref=dst, send_sem=ss, recv_sem=rs,
            device_id=dev, device_id_type=pl.DeviceIdType.MESH,
        )

    def got(dst, rs):
        send(dst, dst, s_ring, rs, (dp, ce)).wait_recv()

    def sent(src, ss):
        send(src, src, ss, r_asg, (dp, ce)).wait_send()

    def slot(b, k):
        p = pair if b == 0 else 1 - pair
        return 2 * p + (h if k == 0 else 1 - h)

    def zof(d, s):
        return (z + NZ - s) % NZ if d == 0 else (z + s) % NZ

    def za_rows(d, s):
        return pl.ds(0, HEAD) if s < 4 else pl.ds(d * (HEAD // 2), HEAD // 2)

    def zb_rows(d, s):
        n = ROWS - HEAD
        return pl.ds(HEAD, n) if s < 4 else pl.ds(HEAD + d * (n // 2), n // 2)

    def za(d, s, b, k):
        where = e.at[zof(d, s - 1), slot(b, k), za_rows(d, s)]
        src = emb.at[za_rows(d, s)] if (s, b, k) == (1, 0, 0) else where
        return send(src, where, s_ring, r_za.at[d, s - 1, b, k], at(x, q, y, zof(1 - d, 1)))

    def za_got(d, s, b, k):
        got(e.at[zof(d, s), slot(b, k), za_rows(d, s)], r_za.at[d, s - 1, b, k])

    def zb(d, s, k):
        where = e.at[zof(d, s - 1), slot(0, k), zb_rows(d, s)]
        src = emb.at[zb_rows(d, s)] if (s, k) == (1, 0) else where
        return send(src, where, s_ring, r_zb.at[d, s - 1, k], at(x, q, y, zof(1 - d, 1)))

    def zb_got(d, s, k):
        got(e.at[zof(d, s), slot(0, k), zb_rows(d, s)], r_zb.at[d, s - 1, k])

    def ya(k):
        where = e.at[z, slot(0, k), pl.ds(0, HEAD)]
        src = emb.at[pl.ds(0, HEAD)] if k == 0 else where
        return send(src, where, s_ring, r_ya.at[k], at(x, q, other_y, z))

    def ya_got(k):
        got(e.at[z, slot(1, k), pl.ds(0, HEAD)], r_ya.at[k])

    def yb(d, s, k):
        where = e.at[zof(d, s), slot(0, k), zb_rows(d, s)]
        src = emb.at[zb_rows(d, s)] if (s, k) == (0, 0) else where
        return send(src, where, s_ring, r_yb.at[d, s, k], at(x, q, other_y, z))

    def yb_got(d, s, k):
        got(e.at[zof(d, s), slot(1, k), zb_rows(d, s)], r_yb.at[d, s, k])

    def la(d, s):
        where = e.at[zof(d, s), :, pl.ds(0, HEAD)]
        return send(where, where, s_l, r_la.at[d, s], at(x, 1 - q, y, z))

    def lb(d, s):
        where = e.at[zof(d, s), :, pl.ds(HEAD, ROWS - HEAD)]
        return send(where, where, s_l, r_lb.at[d, s], at(x, 1 - q, y, z))

    def l4z():
        where = e.at[zof(0, 4), pl.ds(2 * pair, 2), pl.ds(HEAD, ROWS - HEAD)]
        return send(where, where, s_l, r_lb.at[0, 4], at(x, 1 - q, y, z))

    def l4y(d, k):
        where = e.at[zof(d, 4), slot(1, k), zb_rows(d, 4)]
        return send(where, where, s_l, r_l4.at[d, k], at(x, 1 - q, y, z))

    def dirs(s):
        return (0,) if s in (0, 4) else (0, 1)

    def blocks(s):
        return (0, 1) if s == 0 else (2 * s - 1, min(2 * s + 1, NZ))

    def zon(n):
        far = (n + 1) // 2
        return (z + NZ + far * (1 - 2 * (n % 2))) % NZ

    def sel_send(n, k, y_to):
        zo = zon(n)
        to = at(SLOT_Y[k], zo // 4, y_to, z)
        same = (to[0] == dp) & (to[1] == ce)
        src, dst = sel.at[zo, k], rows.at[group, zo % 4]

        @pl.when(jnp.logical_not(same))
        def _():
            send(src, dst, s_sel, r_sel, to).start()

        @pl.when(same)
        def _():
            pltpu.make_async_copy(src, dst, r_sel).start()

    def ids_send(n, y_to):
        to = at(n // 2, n % 2, y_to, z)
        same = (to[0] == dp) & (to[1] == ce)

        @pl.when(jnp.logical_not(same))
        def _():
            send(ids_out, ids_in.at[group], s_ids, r_ids, to).start()

        @pl.when(same)
        def _():
            pltpu.make_async_copy(ids_out, ids_in.at[group], r_ids).start()

    def choose(a_ref, y_to):
        a = a_ref[...] - CENT * (NZ * y_to + z)
        mask = (a >= 0) & (a < CENT)
        m = jnp.where(mask, 1.0, 0.0).astype(F32)
        mb = m.astype(BF16)
        i0 = lax.broadcasted_iota(jnp.int32, (128, 128), 0)
        i1 = lax.broadcasted_iota(jnp.int32, (128, 128), 1)
        before = dot(mb, jnp.where(i0 < i1, 1.0, 0.0).astype(BF16), NN)
        total = dot(mb, jnp.ones((128, 128), BF16), NN)
        v = jnp.where(mask, a + 1, 0)
        high, low = (v // 32).astype(F32), (v % 32).astype(F32)
        first = lax.broadcasted_iota(jnp.int32, (8, 128), 0) == 0
        rank_of = lax.broadcasted_iota(jnp.int32, (128, 128), 0).astype(F32)
        off = (CAP * h).astype(F32)
        run = jnp.zeros((1, 128), F32)
        ids = jnp.zeros((8, 128), F32)
        for i in range(8):
            here = m[i : i + 1] > 0.5
            rank = before[i : i + 1] + run
            run = run + total[i : i + 1]
            one = jnp.where((rank == rank_of) & here, 1.0, 0.0).astype(BF16)
            pick[:, 128 * i : 128 * (i + 1)] = one[:CAP]
            put = jnp.where((rank + off == rank_of) & here, 1.0, 0.0).astype(BF16)
            vals = jnp.where(first, high[i : i + 1], low[i : i + 1]).astype(BF16)
            ids = ids + dot(vals, put, NT)
        ids_out[...] = jnp.broadcast_to(32.0 * ids[0:1] + ids[1:2] - 1.0, (8, 128))

    def norms(first, count):
        @pl.loop(0, count)
        def _(i):
            part = jnp.zeros((128, 128), F32)
            r = pl.ds(pl.multiple_of((first + i) % NX * 128, 128), 128)
            for k in range(FEAT // 128):
                v = c[r, k * 128 : (k + 1) * 128].astype(F32)
                part = part + v * v
            hn[r, :] = 0.5 * jnp.sum(part, axis=1, keepdims=True)

    def choose_rows(lo, hi, y_to):
        @pl.loop(lo, hi)
        def _(n):
            zo = zon(n)
            for k in range(4):
                sel[zo, k] = dot(pick[...], e[zo, k], NN).astype(BF16)
                sel_send(n, k, y_to)

    def score(lo, hi):
        def one(n):
            zo = zon(n)
            left = jnp.concatenate(
                [c[:, pl.ds(pl.multiple_of(yy * 1024 + zo * 128, 128), 128)] for yy in SLOT_Y], axis=1
            )
            return dot(left, jnp.concatenate([e[zo, k] for k in range(4)], axis=1), NT)

        if lo == 0:
            acc[...] = one(0)
        else:

            @pl.loop(lo, hi)
            def _(n):
                acc[...] += one(n)

    def top_rows():
        m = jnp.max(acc[...] - hn[...], axis=0, keepdims=True)
        for i in range(8):
            best[i : i + 1, :] = m[:, 128 * i : 128 * (i + 1)]

    barrier = pltpu.get_barrier_semaphore()
    own_slice = pltpu.make_async_copy(cen.at[:, pl.ds(pl.multiple_of(dp * SLICE, SLICE), SLICE)], cs, l_cs)
    own_asg = pltpu.make_async_copy(asg_hbm, asg, l_asg)
    own_prior = pltpu.make_async_copy(prior_hbm, prior, l_prior)
    own_asg.start()
    own_prior.start()
    own_slice.start()
    peers = [((dp + k) % 8, NZ * yy + z) for k in range(8) for yy in (y, across) if not (k == 0 and yy is y)]
    peers += [(dp, NZ * y + (z + k) % NZ) for k in range(1, NZ)]
    peers += [(dp, NZ * other_y + z), (dp, NZ * (3 - other_y) + z)]
    for to in peers:
        pl.semaphore_signal(barrier, inc=1, device_id=to, device_id_type=pl.DeviceIdType.MESH)
    pl.semaphore_wait(barrier, len(peers))

    def tell(act):
        for yy in range(NY):

            @pl.when(yy != y)
            def _():
                cp = send(best_y.at[y % 2], best_y.at[y % 2], s_by.at[yy], r_by.at[y % 2], at(x, q, yy, z))
                cp.start() if act == "start" else cp.wait_send()

    @pl.when(is_hub)
    def _():
        own = pltpu.make_async_copy(emb, e.at[z, slot(0, 0)], l_own)
        all_c = pltpu.make_async_copy(cen, c, l_c)
        give_asg = send(asg, asg_in, s_asg, r_asg, at(x, 1 - q, y, z))
        for d in (0, 1):
            zb(d, 1, 0).start()
        for d in (0, 1):
            za(d, 1, 0, 0).start()
        ya(0).start()
        yb(0, 0, 0).start()
        own.start()
        all_c.start()
        own_asg.wait()
        give_asg.start()
        got(e.at[z, slot(0, 1), pl.ds(0, HEAD)], r_ext.at[0])
        ya(1).start()
        for d in (0, 1):
            za(d, 1, 0, 1).start()
        ya_got(0)
        for d in (0, 1):
            za(d, 1, 1, 0).start()
        got(e.at[z, slot(0, 1), pl.ds(HEAD, ROWS - HEAD)], r_ext.at[1])
        for d in (0, 1):
            zb(d, 1, 1).start()
        yb(0, 0, 1).start()
        ya_got(1)
        for d in (0, 1):
            za(d, 1, 1, 1).start()
        own.wait()
        la(0, 0).start()
        def finish(s):
            for d in dirs(s):
                for k in (0, 1):
                    yb_got(d, s, k)
                lb(d, s).start()
            choose_rows(*blocks(s), y)
            score(*blocks(s))

        for s in range(1, 5):
            for k in (0, 1):
                for d in (0, 1):
                    zb_got(d, s, k)
                    if s < 4:
                        zb(d, s + 1, k).start()
                    yb(d, s, k).start()
            if s == 1:
                choose(asg, y)
                for n in range(8):
                    ids_send(n, y)
            if s == 4:
                l4z().start()
                finish(3)
            for b, k in ((0, 0), (0, 1), (1, 0), (1, 1)):
                for d in (0, 1):
                    za_got(d, s, b, k)
                    if s < 4:
                        za(d, s + 1, b, k).start()
            for d in dirs(s):
                la(d, s).start()
            if s == 1:
                all_c.wait()
                norms(0, NX)
            if s < 4:
                finish(s - 1)
        for k in (0, 1):
            for d in (0, 1):
                yb_got(d, 4, k)
                l4y(d, k).start()
        score(*blocks(4))
        top_rows()
        got(best_leaf, r_bl)
        best_z[z] = jnp.maximum(best[...], best_leaf[...])
        for k in range(1, NZ):
            send(best_z.at[z], best_z.at[z], s_bz, r_bz, at(x, q, y, (z + k) % NZ)).start()
        choose_rows(*blocks(4), y)
        sent(e.at[:, :, pl.ds(0, 960)], s_ring)
        sent(e, s_l)
        sent(asg, s_asg)
        got(best_z.at[pl.ds(0, NZ - 1)], r_bz)
        m = best_z[0]
        for k in range(1, NZ):
            m = jnp.maximum(m, best_z[k])
        best_y[y % 2] = m
        tell("start")

    @pl.when(jnp.logical_not(is_hub))
    def _():
        def ext(n):
            r = pl.ds(0, HEAD) if n == 0 else pl.ds(HEAD, ROWS - HEAD)
            return send(emb.at[r], e.at[z, slot(0, 0), r], s_ext.at[n], r_ext.at[n], at(x, q, across, z))

        def part(n, k):
            return pl.ds(pl.multiple_of(((x + n) % NX) * QUART + k * PIECE, PIECE), PIECE)

        def cross(k):
            return send(cen.at[part(0, k)], c.at[part(0, k)], s_c, r_cc.at[k], at(x, 1 - q, across, z))

        def near(d, k):
            to = at((x + 1 + 2 * d) % NX, q, y, z)
            return send(c.at[part(0, k)], c.at[part(0, k)], s_c, r_x1.at[d, k], to)

        def far(k):
            d = k // (PIECES // 2)
            to = at((x + 1 + 2 * d) % NX, q, y, z)
            which = part(3 - 2 * d, k)
            return send(c.at[which], c.at[which], s_c, r_x2.at[k], to)

        ext(0).start()
        ext(1).start()
        own_asg.wait()
        for n in (0, 1):
            ext(n).wait_send()
        for k in range(PIECES):
            cross(k).start()
        got(asg_in, r_asg)
        choose(asg_in, across)
        for n in range(8):
            ids_send(n, across)

        def pass_on(k):
            for d in (0, 1):
                got(c.at[part(3 - 2 * d, k)], r_x1.at[d, k])
            far(k).start()

        def arrived(s):
            for d in dirs(s):
                got(e.at[zof(d, s), :, pl.ds(0, HEAD)], r_la.at[d, s])
                if s < 4:
                    got(e.at[zof(d, s), :, pl.ds(HEAD, ROWS - HEAD)], r_lb.at[d, s])
                else:
                    got(e.at[zof(0, 4), pl.ds(2 * pair, 2), pl.ds(HEAD, ROWS - HEAD)], r_lb.at[0, 4])
                    for k in (0, 1):
                        for dd in (0, 1):
                            got(e.at[zof(dd, 4), slot(1, k), zb_rows(dd, 4)], r_l4.at[dd, k])
            if s < 4:
                choose_rows(*blocks(s), across)

        for k in range(PIECES):
            got(c.at[part(0, k)], r_cc.at[k])
            for d in (0, 1):
                near(d, k).start()
            if k > 1:
                pass_on(k - 2)
        arrived(0)
        for k in range(PIECES - 2, PIECES):
            pass_on(k)
        norms(x, 2)
        norms(x + 3, 1)
        arrived(1)
        arrived(2)
        for k in range(PIECES):
            got(c.at[part(2, k)], r_x2.at[k])
        norms(x + 2, 1)
        score(0, 1)
        score(1, 5)
        for s in (3, 4):
            arrived(s)
            score(*blocks(s))
        top_rows()
        give = send(best, best_leaf, s_bl, r_bl, at(x, 1 - q, y, z))
        give.start()
        choose_rows(*blocks(4), across)
        sent(c, s_c)
        give.wait_send()

    own_slice.wait()
    own_prior.wait()
    pr = prior[...].astype(F32)
    got(ids_in, r_ids)
    k_of = lax.broadcasted_iota(jnp.int32, (CENT, 128), 0).astype(F32)
    hot = jnp.concatenate(
        [
            jnp.where(jnp.maximum(ids_in[2 * n, 0:1], ids_in[2 * n + 1, 0:1]) == k_of, 1.0, 0.0).astype(BF16)
            for n in range(4)
        ],
        axis=1,
    )
    counts = dot(jnp.ones((8, SLICE), BF16), hot, NT)
    den[...] = pr + counts[0:1]
    got(rows, r_sel)
    for k in range(4):
        f = slice(k * 128, (k + 1) * 128)
        taken = jnp.concatenate([rows[n, k] for n in range(8)], axis=0)
        num[f, :] = pr * cs[:, f].astype(F32).T + dot(taken.T, hot, NT)

    @pl.when(is_hub)
    def _():
        sent(sel.at[pl.ds(0, NZ - 1)], s_sel)
        sent(ids_in.at[pl.ds(0, 7)], s_ids)
        sent(best_z.at[pl.ds(0, NZ - 1)], s_bz)
        got(best_y.at[1 - y % 2], r_by.at[1 - y % 2])
        tell("wait")

    @pl.when(jnp.logical_not(is_hub))
    def _():
        sent(sel, s_sel)
        sent(ids_in, s_ids)
        for n in (0, 1):
            got(best_y.at[n], r_by.at[n])

    top[...] = jnp.maximum(best_y[0], best_y[1])


def on_device(embeddings, centroids, assignment, prior_counts):
    dma = pltpu.SemaphoreType.DMA
    both = lambda *shape: [dma(shape), dma(shape)]
    vmem, hbm = pl.BlockSpec(memory_space=pltpu.VMEM), pl.BlockSpec(memory_space=pltpu.HBM)
    placed = (embeddings, centroids, assignment.reshape(8, 128), prior_counts.reshape(1, CENT))
    placed = [pltpu.with_memory_space_constraint(v, pltpu.HBM) for v in placed]
    top, num, den = pl.pallas_call(
        kernel,
        out_shape=[
            jax.ShapeDtypeStruct((8, 128), F32),
            jax.ShapeDtypeStruct((SLICE, CENT), F32),
            jax.ShapeDtypeStruct((1, CENT), F32),
        ],
        in_specs=[hbm, hbm, hbm, hbm],
        out_specs=[vmem, vmem, vmem],
        scratch_shapes=[
            pltpu.VMEM((NZ, 4, ROWS, WIDTH), BF16),
            pltpu.VMEM((CENT, FEAT), BF16),
            pltpu.VMEM((CENT, ROWS), F32),
            pltpu.VMEM((CENT, SLICE), BF16),
            pltpu.VMEM((NZ, 4, CAP, WIDTH), BF16),
            pltpu.VMEM((8, 4, CAP, WIDTH), BF16),
            pltpu.VMEM((8, 128), F32),
            pltpu.VMEM((8, 8, 128), F32),
            pltpu.VMEM((8, 128), jnp.int32),
            pltpu.VMEM((8, 128), jnp.int32),
            pltpu.VMEM((1, CENT), jnp.int32),
            pltpu.VMEM((CAP, ROWS), BF16),
            pltpu.VMEM((CENT, 1), F32),
            pltpu.VMEM((8, 128), F32),
            pltpu.VMEM((8, 128), F32),
            pltpu.VMEM((NZ, 8, 128), F32),
            pltpu.VMEM((2, 8, 128), F32),
            dma(()), dma((2, 4, 2, 2)), dma((2, 4, 2)), dma((2,)), dma((2, 5, 2)),
            *both(2),
            dma(()), dma((2, 5)), dma((2, 5)), dma((2, 2)),
            dma(()), dma((PIECES,)), dma((2, PIECES)), dma((PIECES,)),
            *both(), *both(),
            *both(), *both(),
            dma((4,)), dma((2,)),
            *both(),
            *both(), *both(), dma(()),
        ],
        compiler_params=pltpu.CompilerParams(
            collective_id=0, has_side_effects=True, vmem_limit_bytes=40 * 2**20
        ),
        name="score_and_update",
    )(*placed)
    return top.reshape(ROWS), num / den


def solution(mesh):
    placed = (P("dp", "cent"), P("cent", None), P("dp"), P("cent"))
    return jax.shard_map(
        on_device, mesh=mesh, in_specs=placed, out_specs=(P("dp"), P("dp", "cent")), check_vma=False
    )
```

```python
import jax
import jax.numpy as jnp
from jax import lax
from jax.experimental import pallas as pl
from jax.experimental.pallas import tpu as pltpu
from jax.sharding import PartitionSpec as P

NX, NY, NZ = 4, 4, 8
ROWS = 1024
WIDTH = 128
CENT = 512
FEAT = 4096
CAP = 64
SLICE = 512
HEAD = 416
STAGES = 0, 384, 640, 1024
QUART = CENT // NX
PIECES = 8
PIECE = QUART // PIECES
SLOT_Y = (0, 3, 1, 2)
F32, BF16 = jnp.float32, jnp.bfloat16
NT = (((1,), (1,)), ((), ()))
NN = (((1,), (0,)), ((), ()))


def dot(a, b, dims):
    return lax.dot_general(a, b, dims, preferred_element_type=F32)


def kernel(
    emb, cen, asg_hbm, prior_hbm, top, num, den,
    e, c, acc, cs, sel, rows, ids_out, ids_in, asg, prior, pick, hn, best, best_y,
    s_ring, r_za, r_zb, r_ya, r_yb, s_ext, r_ext, s_l, r_la, r_lb, r_l4,
    s_c, r_cc, r_x1, r_x2, s_sel, r_sel, s_ids, r_ids, s_pick, r_pick, s_pick_ids, r_pick_ids, s_by, r_by,
    l_own, l_c, l_cs, l_asg, l_prior,
):
    dp, ce = lax.axis_index("dp"), lax.axis_index("cent")
    x, q, y, z = dp // 2, dp % 2, ce // NZ, ce % NZ
    h = y // 2
    pair = ((y + 1) // 2) % 2
    other_y, across = y + 1 - 2 * (y % 2), 3 - y
    group = 2 * x + h
    is_hub = q == h

    def at(x_, q_, y_, z_):
        return (2 * x_ + q_, NZ * y_ + z_)

    def send(src, dst, ss, rs, dev):
        return pltpu.make_async_remote_copy(
            src_ref=src, dst_ref=dst, send_sem=ss, recv_sem=rs,
            device_id=dev, device_id_type=pl.DeviceIdType.MESH,
        )

    def got(dst, rs):
        send(dst, dst, s_ring, rs, (dp, ce)).wait_recv()

    def sent(src, ss):
        send(src, src, ss, r_pick, (dp, ce)).wait_send()

    def slot(b, k):
        p = pair if b == 0 else 1 - pair
        if k is None:
            return pl.ds(2 * p, 2)
        return 2 * p + (h if k == 0 else 1 - h)

    def zof(d, s):
        return (z + NZ - s) % NZ if d == 0 else (z + s) % NZ

    def zon(n):
        far = (n + 1) // 2
        return (z + NZ + far * (1 - 2 * (n % 2))) % NZ

    def dirs(s):
        return (0,) if s in (0, 4) else (0, 1)

    def za_rows(d, s):
        return pl.ds(0, HEAD) if s < 4 else pl.ds(d * (HEAD // 2), HEAD // 2)

    def zb_rows(d, s):
        n = ROWS - HEAD
        return pl.ds(HEAD, n) if s < 4 else pl.ds(HEAD + d * (n // 2), n // 2)

    def za(d, s, b, k):
        where = e.at[zof(d, s - 1), slot(b, k), za_rows(d, s)]
        src = emb.at[za_rows(d, s)] if (s, b, k) == (1, 0, 0) else where
        return send(src, where, s_ring, r_za.at[d, s - 1, b, k or 0], at(x, q, y, zof(1 - d, 1)))

    def za_got(d, s, b, k):
        got(e.at[zof(d, s), slot(b, k), za_rows(d, s)], r_za.at[d, s - 1, b, k or 0])

    def zb(d, s, k):
        where = e.at[zof(d, s - 1), slot(0, k), zb_rows(d, s)]
        src = emb.at[zb_rows(d, s)] if (s, k) == (1, 0) else where
        return send(src, where, s_ring, r_zb.at[d, s - 1, k or 0], at(x, q, y, zof(1 - d, 1)))

    def zb_got(d, s, k):
        got(e.at[zof(d, s), slot(0, k), zb_rows(d, s)], r_zb.at[d, s - 1, k or 0])

    def ya(k):
        where = e.at[z, slot(0, k), pl.ds(0, HEAD)]
        src = emb.at[pl.ds(0, HEAD)] if k == 0 else where
        return send(src, where, s_ring, r_ya.at[k], at(x, q, other_y, z))

    def ya_got(k):
        got(e.at[z, slot(1, k), pl.ds(0, HEAD)], r_ya.at[k])

    def yb(d, s, k):
        where = e.at[zof(d, s), slot(0, k), zb_rows(d, s)]
        src = emb.at[zb_rows(d, s)] if (s, k) == (0, 0) else where
        return send(src, where, s_ring, r_yb.at[d, s, k or 0], at(x, q, other_y, z))

    def yb_got(d, s, k):
        got(e.at[zof(d, s), slot(1, k), zb_rows(d, s)], r_yb.at[d, s, k or 0])

    def to_leaf(where, rs):
        return send(where, where, s_l, rs, at(x, 1 - q, y, z))

    def la_where(d, s):
        return e.at[zof(d, s), :, pl.ds(0, HEAD)]

    def lb_where(d, s):
        return e.at[zof(d, s), :, pl.ds(HEAD, ROWS - HEAD)]

    def l4z_where():
        return e.at[zof(0, 4), slot(0, None), pl.ds(HEAD, ROWS - HEAD)]

    def l4y_where(d):
        return e.at[zof(d, 4), slot(1, None), zb_rows(d, 4)]

    def send_or_keep(src, dst, ss, rs, to):
        same = (to[0] == dp) & (to[1] == ce)

        @pl.when(jnp.logical_not(same))
        def _():
            send(src, dst, ss, rs, to).start()

        @pl.when(same)
        def _():
            pltpu.make_async_copy(src, dst, rs).start()

    def choose(t, y_to):
        a = asg[...] - CENT * (NZ * y_to + z)
        mask = (a >= 0) & (a < CENT)
        m = jnp.where(mask, 1.0, 0.0).astype(F32)
        mb = m.astype(BF16)
        i0 = lax.broadcasted_iota(jnp.int32, (128, 128), 0)
        i1 = lax.broadcasted_iota(jnp.int32, (128, 128), 1)
        before = dot(mb, jnp.where(i0 < i1, 1.0, 0.0).astype(BF16), NN)
        total = dot(mb, jnp.ones((128, 128), BF16), NN)
        v = jnp.where(mask, a + 1, 0)
        high, low = (v // 32).astype(F32), (v % 32).astype(F32)
        first = lax.broadcasted_iota(jnp.int32, (8, 128), 0) == 0
        rank_of = lax.broadcasted_iota(jnp.int32, (128, 128), 0).astype(F32)
        off = (CAP * h).astype(F32)
        run = jnp.zeros((1, 128), F32)
        ids = jnp.zeros((8, 128), F32)
        for i in range(8):
            here = m[i : i + 1] > 0.5
            rank = before[i : i + 1] + run
            run = run + total[i : i + 1]
            one = jnp.where((rank == rank_of) & here, 1.0, 0.0).astype(BF16)
            pick[CAP * t : CAP * (t + 1), 128 * i : 128 * (i + 1)] = one[:CAP]
            put = jnp.where((rank + off == rank_of) & here, 1.0, 0.0).astype(BF16)
            vals = jnp.where(first, high[i : i + 1], low[i : i + 1]).astype(BF16)
            ids = ids + dot(vals, put, NT)
        ids_out[t] = jnp.broadcast_to(32.0 * ids[0:1] + ids[1:2] - 1.0, (8, 128))

    def norms(first, count, base):
        @pl.loop(0, count)
        def _(i):
            part = jnp.zeros((128, 128), F32)
            r = pl.ds(pl.multiple_of(base + (first + i) % NX * 128, 128), 128)
            for k in range(FEAT // 128):
                v = c[r, k * 128 : (k + 1) * 128].astype(F32)
                part = part + v * v
            hn[r, :] = 0.5 * jnp.sum(part, axis=1, keepdims=True)

    def choose_rows(n):
        zo = zon(n)
        for k in range(4):
            got_rows = dot(pick[...], e[zo, k], NN).astype(BF16)
            for t in (0, 1):
                sel[t, k, zo] = got_rows[CAP * t : CAP * (t + 1)]

    def give_rows(n):
        zo = zon(n)

        def go():
            for k in range(4):
                for t in (0, 1):
                    to = at(SLOT_Y[k], zo // 4, across if t else y, z)
                    src, dst = sel.at[t, k, zo], rows.at[group, zo % 4]
                    if t:
                        send(src, dst, s_sel.at[t], r_sel, to).start()
                    else:
                        send_or_keep(src, dst, s_sel.at[t], r_sel, to)

        if n == NZ - 1:
            go()
        else:
            pl.when(zo // 4 != z // 4)(go)

    def give_half():
        half = z // 4
        for k in range(4):
            for t in (0, 1):
                to = at(SLOT_Y[k], half, across if t else y, z)
                src, dst = sel.at[t, k, pl.ds(4 * half, 4)], rows.at[group]
                if t:
                    send(src, dst, s_sel.at[t], r_sel, to).start()
                else:
                    send_or_keep(src, dst, s_sel.at[t], r_sel, to)

    def product(n, r, cr):
        zo = zon(n)
        left = jnp.concatenate(
            [c[cr, pl.ds(pl.multiple_of(yy * 1024 + zo * 128, 128), 128)] for yy in SLOT_Y], axis=1
        )
        return dot(left, jnp.concatenate([e[zo, k, r] for k in range(4)], axis=1), NT)

    def score(n, t):
        cr = slice(CENT * t, CENT * (t + 1))
        if n == 0:
            acc[cr] = product(0, slice(None), cr)
        else:
            acc[cr] += product(n, slice(None), cr)

    def last_score(stage):
        lo, hi = STAGES[stage : stage + 2]
        r = slice(lo, hi)
        m = jnp.max(acc[:, r] + product(NZ - 1, r, slice(None)) - hn[...], axis=0, keepdims=True)
        for i in range(lo // 128, hi // 128):
            best[i : i + 1, :] = m[:, 128 * i - lo : 128 * (i + 1) - lo]

    barrier = pltpu.get_barrier_semaphore()
    own_slice = pltpu.make_async_copy(cen.at[:, pl.ds(pl.multiple_of(dp * SLICE, SLICE), SLICE)], cs, l_cs)
    own_asg = pltpu.make_async_copy(asg_hbm, asg, l_asg)
    own_prior = pltpu.make_async_copy(prior_hbm, prior, l_prior)
    own = pltpu.make_async_copy(emb, e.at[z, slot(0, 0)], l_own)
    own_c = pltpu.make_async_copy(cen, c.at[pl.ds(0, CENT)], l_c)
    own_prior.start()
    own_slice.start()
    peers = [(dp, NZ * y + (z + 1) % NZ), (dp, NZ * y + (z + NZ - 1) % NZ), (dp, NZ * other_y + z)]
    peers += [at(x, 1 - q, y, z), at(x, 1 - q, across, z), (dp, NZ * across + z)]
    peers += [((dp + 2) % 8, ce), ((dp + 6) % 8, ce)]
    for to in peers:
        pl.semaphore_signal(barrier, inc=1, device_id=to, device_id_type=pl.DeviceIdType.MESH)

    @pl.when(is_hub)
    def _():
        own_asg.start()
        own.start()

    @pl.when(jnp.logical_not(is_hub))
    def _():
        own_c.start()

    pl.semaphore_wait(barrier, len(peers))

    @pl.when(is_hub)
    def _():
        for d in (0, 1):
            zb(d, 1, 0).start()
        for d in (0, 1):
            za(d, 1, 0, 0).start()
        ya(0).start()
        yb(0, 0, 0).start()
        got(e.at[z, slot(0, 1), pl.ds(0, HEAD)], r_ext.at[0])
        ya(1).start()
        for d in (0, 1):
            za(d, 1, 0, 1).start()
        ya_got(0)
        for d in (0, 1):
            za(d, 1, 1, 0).start()
        own_asg.wait()
        choose(0, y)
        got(e.at[z, slot(0, 1), pl.ds(HEAD, ROWS - HEAD)], r_ext.at[1])
        for d in (0, 1):
            zb(d, 1, 1).start()
        yb(0, 0, 1).start()
        ya_got(1)
        for d in (0, 1):
            za(d, 1, 1, 1).start()
        own.wait()
        to_leaf(la_where(0, 0), r_la.at[0, 0]).start()
        choose(1, across)
        send(pick, pick, s_pick, r_pick, at(x, 1 - q, y, z)).start()
        send(ids_out, ids_out, s_pick_ids, r_pick_ids, at(x, 1 - q, y, z)).start()

        def y_done(s):
            for d in dirs(s):
                for k in (0, 1) if s < 2 else (None,):
                    yb_got(d, s, k)
                to_leaf(lb_where(d, s), r_lb.at[d, s]).start()

        for k in (0, 1, None):
            for d in (0, 1):
                if k is not None:
                    zb_got(d, 1, k)
                    yb(d, 1, k).start()
                    if k == 1:
                        zb(d, 2, None).start()
            if k == 0:
                for d in (0, 1):
                    for kk in (0, 1):
                        za_got(d, 1, 0, kk)
                    za(d, 2, 0, None).start()
                for d in (0, 1):
                    za_got(d, 1, 1, 0)
            elif k is None:
                for d in (0, 1):
                    za_got(d, 1, 1, 1)
                    za(d, 2, 1, None).start()
        for d in (0, 1):
            to_leaf(la_where(d, 1), r_la.at[d, 1]).start()
        y_done(0)
        for s in range(2, 5):
            for d in (0, 1):
                zb_got(d, s, None)
                if s < 4:
                    zb(d, s + 1, None).start()
                yb(d, s, None).start()
            if s == 4:
                to_leaf(l4z_where(), r_lb.at[0, 4]).start()
            for d in (0, 1):
                za_got(d, s, 0, None)
                if s < 4:
                    za(d, s + 1, 0, None).start()
            y_done(s - 1)
            for d in (0, 1):
                za_got(d, s, 1, None)
                if s < 4:
                    za(d, s + 1, 1, None).start()
            for d in dirs(s):
                to_leaf(la_where(d, s), r_la.at[d, s]).start()
        for d in (0, 1):
            yb_got(d, 4, None)
            to_leaf(l4y_where(d), r_l4.at[d]).start()
        sent(e.at[:, :, pl.ds(0, 960)], s_ring)
        sent(e, s_l)
        sent(pick, s_pick)
        sent(ids_out, s_pick_ids)

    @pl.when(jnp.logical_not(is_hub))
    def _():
        def ext(n):
            r = pl.ds(0, HEAD) if n == 0 else pl.ds(HEAD, ROWS - HEAD)
            return send(emb.at[r], e.at[z, slot(0, 0), r], s_ext.at[n], r_ext.at[n], at(x, q, across, z))

        def part(n, k, base=CENT):
            return pl.ds(pl.multiple_of(base + ((x + n) % NX) * QUART + k * PIECE, PIECE), PIECE)

        def cross(k):
            return send(cen.at[part(0, k, 0)], c.at[part(0, k)], s_c, r_cc.at[k], at(x, 1 - q, across, z))

        def near(d, k):
            to = at((x + 1 + 2 * d) % NX, q, y, z)
            return send(c.at[part(0, k)], c.at[part(0, k)], s_c, r_x1.at[d, k], to)

        def far(k):
            d = k // (PIECES // 2)
            to = at((x + 1 + 2 * d) % NX, q, y, z)
            which = part(3 - 2 * d, k)
            return send(c.at[which], c.at[which], s_c, r_x2.at[k], to)

        def pass_on(k):
            for d in (0, 1):
                got(c.at[part(3 - 2 * d, k)], r_x1.at[d, k])
            far(k).start()

        def arrived(s, n):
            d = n % 2 if s == 0 else (n + 1) % 2
            got(la_where(d, s), r_la.at[d, s])
            got(lb_where(d, s), r_lb.at[d, s])
            choose_rows(n)
            score(n, 0)

        ext(0).start()
        ext(1).start()
        for n in (0, 1):
            ext(n).wait_send()
        for k in range(PIECES):
            cross(k).start()
        own_c.wait()
        norms(0, NX, 0)
        for k in range(PIECES):
            got(c.at[part(0, k)], r_cc.at[k])
            for d in (0, 1):
                near(d, k).start()
            if k > 1:
                pass_on(k - 2)
            if k == 3:
                got(pick, r_pick)
                arrived(0, 0)
        arrived(1, 1)
        for k in range(PIECES - 2, PIECES):
            pass_on(k)
        arrived(1, 2)
        norms(x, 2, CENT)
        norms(x + 3, 1, CENT)
        arrived(2, 3)
        arrived(2, 4)
        for k in range(PIECES):
            got(c.at[part(2, k)], r_x2.at[k])
        got(ids_out, r_pick_ids)
        for n in range(8):
            send_or_keep(ids_out.at[0], ids_in.at[group], s_ids.at[0], r_ids, at(n // 2, n % 2, y, z))
            send(ids_out.at[1], ids_in.at[group], s_ids.at[1], r_ids, at(n // 2, n % 2, across, z)).start()
        for n in range(1, 5):
            give_rows(n)
        norms(x + 2, 1, CENT)
        for n in range(5):
            score(n, 1)
        for n in (5, 6):
            arrived(3, n)
            give_rows(n)
            score(n, 1)
        give_half()
        got(la_where(0, 4), r_la.at[0, 4])
        last_score(0)
        got(l4z_where(), r_lb.at[0, 4])
        for d in (0, 1):
            got(l4y_where(d), r_l4.at[d])
            last_score(d + 1)
        for k in (4, 3, 5, 2, 6, 1, 7, 0):
            for yy in (3 - other_y, across, other_y, y):
                to = at(x, h, yy, (z + k) % NZ)
                send(best, best_y.at[y % 2, z], s_by, r_by, to).start()
        choose_rows(NZ - 1)
        give_rows(NZ - 1)
        sent(c.at[pl.ds(0, CENT)], s_c)

    own_slice.wait()
    own_prior.wait()
    pr = prior[...].astype(F32)
    got(ids_in, r_ids)
    k_of = lax.broadcasted_iota(jnp.int32, (CENT, 128), 0).astype(F32)
    hot = jnp.concatenate(
        [
            jnp.where(jnp.maximum(ids_in[2 * n, 0:1], ids_in[2 * n + 1, 0:1]) == k_of, 1.0, 0.0).astype(BF16)
            for n in range(4)
        ],
        axis=1,
    )
    counts = dot(jnp.ones((8, SLICE), BF16), hot, NT)
    den[...] = pr + counts[0:1]
    for k in range(4):
        f = slice(k * 128, (k + 1) * 128)
        num[f, :] = pr * cs[:, f].astype(F32).T
    got(rows, r_sel)
    for k in range(4):
        f = slice(k * 128, (k + 1) * 128)
        taken = jnp.concatenate([rows[n, k] for n in range(8)], axis=0)
        num[f, :] += dot(taken.T, hot, NT)

    @pl.when(jnp.logical_not(is_hub))
    def _():
        sent(sel.at[0, :, pl.ds(0, NZ - 1)], s_sel.at[0])
        sent(sel.at[1], s_sel.at[1])
        sent(ids_in.at[pl.ds(0, 7)], s_ids.at[0])
        sent(ids_in, s_ids.at[1])
        sent(e.at[0, 0, pl.ds(0, 512)], s_by)

    got(best_y, r_by)
    m = best_y[0, 0]
    for n in range(1, 2 * NZ):
        m = jnp.maximum(m, best_y[n // NZ, n % NZ])
    top[...] = m


def on_device(embeddings, centroids, assignment, prior_counts):
    dma = pltpu.SemaphoreType.DMA
    both = lambda *shape: [dma(shape), dma(shape)]
    vmem, hbm = pl.BlockSpec(memory_space=pltpu.VMEM), pl.BlockSpec(memory_space=pltpu.HBM)
    placed = (embeddings, centroids, assignment.reshape(8, 128), prior_counts.reshape(1, CENT))
    placed = [pltpu.with_memory_space_constraint(v, pltpu.HBM) for v in placed]
    top, num, den = pl.pallas_call(
        kernel,
        out_shape=[
            jax.ShapeDtypeStruct((8, 128), F32),
            jax.ShapeDtypeStruct((SLICE, CENT), F32),
            jax.ShapeDtypeStruct((1, CENT), F32),
        ],
        in_specs=[hbm, hbm, hbm, hbm],
        out_specs=[vmem, vmem, vmem],
        scratch_shapes=[
            pltpu.VMEM((NZ, 4, ROWS, WIDTH), BF16),
            pltpu.VMEM((2 * CENT, FEAT), BF16),
            pltpu.VMEM((2 * CENT, ROWS), F32),
            pltpu.VMEM((CENT, SLICE), BF16),
            pltpu.VMEM((2, 4, NZ, CAP, WIDTH), BF16),
            pltpu.VMEM((8, 4, CAP, WIDTH), BF16),
            pltpu.VMEM((2, 8, 128), F32),
            pltpu.VMEM((8, 8, 128), F32),
            pltpu.VMEM((8, 128), jnp.int32),
            pltpu.VMEM((1, CENT), jnp.int32),
            pltpu.VMEM((2 * CAP, ROWS), BF16),
            pltpu.VMEM((2 * CENT, 1), F32),
            pltpu.VMEM((8, 128), F32),
            pltpu.VMEM((2, NZ, 8, 128), F32),
            dma(()), dma((2, 4, 2, 2)), dma((2, 4, 2)), dma((2,)), dma((2, 5, 2)),
            *both(2),
            dma(()), dma((2, 5)), dma((2, 5)), dma((2,)),
            dma(()), dma((PIECES,)), dma((2, PIECES)), dma((PIECES,)),
            dma((2,)), dma(()),
            dma((2,)), dma(()),
            *both(), *both(), *both(),
            *both(), *both(), dma(()),
        ],
        compiler_params=pltpu.CompilerParams(
            collective_id=0, has_side_effects=True, vmem_limit_bytes=40 * 2**20
        ),
        name="score_and_update",
    )(*placed)
    return top.reshape(ROWS), num / den


def solution(mesh):
    placed = (P("dp", "cent"), P("cent", None), P("dp"), P("cent"))
    return jax.shard_map(
        on_device, mesh=mesh, in_specs=placed, out_specs=(P("dp"), P("dp", "cent")), check_vma=False
    )
```

```python
import jax
import jax.numpy as jnp
from jax import lax
from jax.experimental import pallas as pl
from jax.experimental.pallas import tpu as pltpu
from jax.sharding import PartitionSpec as P

NX, NY, NZ = 4, 4, 8
ROWS = 1024
WIDTH = 128
CENT = 512
FEAT = 4096
CAP = 64
SLICE = 512
HEAD = 480
STAGES = 0, 384, 640, 1024
QUART = CENT // NX
PIECES = 8
PIECE = QUART // PIECES
SLOT_Y = (0, 3, 1, 2)
F32, BF16 = jnp.float32, jnp.bfloat16
NT = (((1,), (1,)), ((), ()))
NN = (((1,), (0,)), ((), ()))


def dot(a, b, dims):
    return lax.dot_general(a, b, dims, preferred_element_type=F32)


def kernel(
    emb, cen, asg_hbm, prior_hbm, top, num, den,
    e, c, acc, cs, sel, spare, rows, ids_out, ids_in, asg, prior, pick, hn, best, best_y,
    s_ring, r_za, r_zb, r_ya, r_yb, s_ext, r_ext, s_l, r_la, r_lb, r_l4,
    s_c, r_cc, r_x1, r_x2, s_sel, r_sel, s_ids, r_ids, s_by, r_by,
    l_own, l_c, l_cs, l_asg, l_prior, ready,
):
    dp, ce = lax.axis_index("dp"), lax.axis_index("cent")
    x, q, y, z = dp // 2, dp % 2, ce // NZ, ce % NZ
    h = y // 2
    pair = ((y + 1) // 2) % 2
    other_y, across = y + 1 - 2 * (y % 2), 3 - y
    group = 2 * x + h
    is_hub = q == h

    def at(x_, q_, y_, z_):
        return (2 * x_ + q_, NZ * y_ + z_)

    def send(src, dst, ss, rs, dev):
        return pltpu.make_async_remote_copy(
            src_ref=src, dst_ref=dst, send_sem=ss, recv_sem=rs,
            device_id=dev, device_id_type=pl.DeviceIdType.MESH,
        )

    def got(dst, rs):
        send(dst, dst, s_ring, rs, (dp, ce)).wait_recv()

    def sent(src, ss):
        send(src, src, ss, r_by, (dp, ce)).wait_send()

    def slot(b, k):
        p = pair if b == 0 else 1 - pair
        if k is None:
            return pl.ds(2 * p, 2)
        return 2 * p + (h if k == 0 else 1 - h)

    def zof(d, s):
        return (z + NZ - s) % NZ if d == 0 else (z + s) % NZ

    def zon(n):
        far = (n + 1) // 2
        return (z + NZ + far * (1 - 2 * (n % 2))) % NZ

    def dirs(s):
        return (0,) if s in (0, 4) else (0, 1)

    def za_rows(d, s):
        return pl.ds(0, HEAD) if s < 4 else pl.ds(d * (HEAD // 2), HEAD // 2)

    def zb_rows(d, s):
        n = ROWS - HEAD
        return pl.ds(HEAD, n) if s < 4 else pl.ds(HEAD + d * (n // 2), n // 2)

    def za(d, s, b, k):
        where = e.at[zof(d, s - 1), slot(b, k), za_rows(d, s)]
        src = emb.at[za_rows(d, s)] if (s, b, k) == (1, 0, 0) else where
        return send(src, where, s_ring, r_za.at[d, s - 1, b, k or 0], at(x, q, y, zof(1 - d, 1)))

    def za_got(d, s, b, k):
        got(e.at[zof(d, s), slot(b, k), za_rows(d, s)], r_za.at[d, s - 1, b, k or 0])

    def zb(d, s, k):
        where = e.at[zof(d, s - 1), slot(0, k), zb_rows(d, s)]
        src = emb.at[zb_rows(d, s)] if (s, k) == (1, 0) else where
        return send(src, where, s_ring, r_zb.at[d, s - 1, k or 0], at(x, q, y, zof(1 - d, 1)))

    def zb_got(d, s, k):
        got(e.at[zof(d, s), slot(0, k), zb_rows(d, s)], r_zb.at[d, s - 1, k or 0])

    def ya(k):
        where = e.at[z, slot(0, k), pl.ds(0, HEAD)]
        src = emb.at[pl.ds(0, HEAD)] if k == 0 else where
        return send(src, where, s_ring, r_ya.at[k], at(x, q, other_y, z))

    def ya_got(k):
        got(e.at[z, slot(1, k), pl.ds(0, HEAD)], r_ya.at[k])

    def yb(d, s, k):
        where = e.at[zof(d, s), slot(0, k), zb_rows(d, s)]
        src = emb.at[zb_rows(d, s)] if (s, k) == (0, 0) else where
        return send(src, where, s_ring, r_yb.at[d, s, k or 0], at(x, q, other_y, z))

    def yb_got(d, s, k):
        got(e.at[zof(d, s), slot(1, k), zb_rows(d, s)], r_yb.at[d, s, k or 0])

    def to_leaf(where, rs):
        return send(where, where, s_l, rs, at(x, 1 - q, y, z))

    def la_where(d, s):
        return e.at[zof(d, s), :, pl.ds(0, HEAD)]

    def lb_where(d, s):
        return e.at[zof(d, s), :, pl.ds(HEAD, ROWS - HEAD)]

    def l4z_where():
        return e.at[zof(0, 4), slot(0, None), pl.ds(HEAD, ROWS - HEAD)]

    def l4y_where(d):
        return e.at[zof(d, 4), slot(1, None), zb_rows(d, 4)]

    def send_or_keep(src, dst, ss, rs, to, spare=None):
        same = (to[0] == dp) & (to[1] == ce)

        @pl.when(jnp.logical_not(same))
        def _():
            send(src, dst, ss, rs, to).start()

        @pl.when(same)
        def _():
            pltpu.make_async_copy(src, dst, rs).start()
            if spare is not None:
                pltpu.make_async_copy(src, spare, ss).start()

    def choose(t, y_to):
        a = asg[...] - CENT * (NZ * y_to + z)
        mask = (a >= 0) & (a < CENT)
        m = jnp.where(mask, 1.0, 0.0).astype(F32)
        mb = m.astype(BF16)
        i0 = lax.broadcasted_iota(jnp.int32, (128, 128), 0)
        i1 = lax.broadcasted_iota(jnp.int32, (128, 128), 1)
        before = dot(mb, jnp.where(i0 < i1, 1.0, 0.0).astype(BF16), NN)
        total = dot(mb, jnp.ones((128, 128), BF16), NN)
        v = jnp.where(mask, a + 1, 0)
        high, low = (v // 32).astype(F32), (v % 32).astype(F32)
        first = lax.broadcasted_iota(jnp.int32, (8, 128), 0) == 0
        rank_of = lax.broadcasted_iota(jnp.int32, (128, 128), 0).astype(F32)
        off = (CAP * h).astype(F32)
        run = jnp.zeros((1, 128), F32)
        ids = jnp.zeros((8, 128), F32)
        for i in range(8):
            here = m[i : i + 1] > 0.5
            rank = before[i : i + 1] + run
            run = run + total[i : i + 1]
            one = jnp.where((rank == rank_of) & here, 1.0, 0.0).astype(BF16)
            pick[CAP * t : CAP * (t + 1), 128 * i : 128 * (i + 1)] = one[:CAP]
            put = jnp.where((rank + off == rank_of) & here, 1.0, 0.0).astype(BF16)
            vals = jnp.where(first, high[i : i + 1], low[i : i + 1]).astype(BF16)
            ids = ids + dot(vals, put, NT)
        ids_out[t] = jnp.broadcast_to(32.0 * ids[0:1] + ids[1:2] - 1.0, (8, 128))

    def norms(first, count, base):
        @pl.loop(0, count)
        def _(i):
            part = jnp.zeros((128, 128), F32)
            r = pl.ds(pl.multiple_of(base + (first + i) % NX * 128, 128), 128)
            for k in range(FEAT // 128):
                v = c[r, k * 128 : (k + 1) * 128].astype(F32)
                part = part + v * v
            hn[r, :] = 0.5 * jnp.sum(part, axis=1, keepdims=True)

    def choose_rows(n):
        zo = zon(n)
        for k in range(4):
            got_rows = dot(pick[...], e[zo, k], NN).astype(BF16)
            for t in (0, 1):
                sel[t, k, zo] = got_rows[CAP * t : CAP * (t + 1)]

    def give_rows(n):
        zo = zon(n)
        for k in range(4):
            for t in (0, 1):
                to = at(SLOT_Y[k], zo // 4, across if t else y, z)
                src, dst = sel.at[t, k, zo], rows.at[group, zo % 4]
                if t:
                    send(src, dst, s_sel.at[t], r_sel, to).start()
                else:
                    send_or_keep(src, dst, s_sel.at[t], r_sel, to, spare.at[n])

    def product(n, r, cr):
        zo = zon(n)
        left = jnp.concatenate(
            [c[cr, pl.ds(pl.multiple_of(yy * 1024 + zo * 128, 128), 128)] for yy in SLOT_Y], axis=1
        )
        return dot(left, jnp.concatenate([e[zo, k, r] for k in range(4)], axis=1), NT)

    def score(n, t):
        cr = slice(CENT * t, CENT * (t + 1))
        if n == 0:
            acc[cr] = product(0, slice(None), cr)
        else:
            acc[cr] += product(n, slice(None), cr)

    def last_score(stage):
        lo, hi = STAGES[stage : stage + 2]
        r = slice(lo, hi)
        m = jnp.max(acc[:, r] + product(NZ - 1, r, slice(None)) - hn[...], axis=0, keepdims=True)
        for i in range(lo // 128, hi // 128):
            best[i : i + 1, :] = m[:, 128 * i - lo : 128 * (i + 1) - lo]

    barrier = pltpu.get_barrier_semaphore()
    own_slice = pltpu.make_async_copy(cen.at[:, pl.ds(pl.multiple_of(dp * SLICE, SLICE), SLICE)], cs, l_cs)
    own_asg = pltpu.make_async_copy(asg_hbm, asg, l_asg)
    own_prior = pltpu.make_async_copy(prior_hbm, prior, l_prior)
    own = pltpu.make_async_copy(emb, e.at[z, slot(0, 0)], l_own)
    own_c = pltpu.make_async_copy(cen, c.at[pl.ds(0, CENT)], l_c)
    own_prior.start()
    own_slice.start()
    peers = [(dp, NZ * y + (z + 1) % NZ), (dp, NZ * y + (z + NZ - 1) % NZ), (dp, NZ * other_y + z)]
    peers += [at(x, 1 - q, y, z), at(x, 1 - q, across, z), (dp, NZ * across + z)]
    peers += [((dp + 2) % 8, ce), ((dp + 6) % 8, ce)]
    for to in peers:
        pl.semaphore_signal(barrier, inc=1, device_id=to, device_id_type=pl.DeviceIdType.MESH)

    @pl.when(is_hub)
    def _():
        own_asg.start()
        own.start()

    @pl.when(jnp.logical_not(is_hub))
    def _():
        own_c.start()

    pl.semaphore_wait(barrier, len(peers))

    @pl.when(is_hub)
    def _():
        for d in (0, 1):
            zb(d, 1, 0).start()
        for d in (0, 1):
            za(d, 1, 0, 0).start()
        ya(0).start()
        yb(0, 0, 0).start()
        got(e.at[z, slot(0, 1), pl.ds(0, HEAD)], r_ext.at[0])
        ya(1).start()
        for d in (0, 1):
            za(d, 1, 0, 1).start()
        ya_got(0)
        for d in (0, 1):
            za(d, 1, 1, 0).start()
        own_asg.wait()
        choose(0, y)
        got(e.at[z, slot(0, 1), pl.ds(HEAD, ROWS - HEAD)], r_ext.at[1])
        for d in (0, 1):
            zb(d, 1, 1).start()
        yb(0, 0, 1).start()
        ya_got(1)
        for d in (0, 1):
            za(d, 1, 1, 1).start()
        own.wait()
        to_leaf(la_where(0, 0), r_la.at[0, 0]).start()
        choose(1, across)

        def y_done(s):
            for d in dirs(s):
                for k in (0, 1) if s < 2 else (None,):
                    yb_got(d, s, k)
                to_leaf(lb_where(d, s), r_lb.at[d, s]).start()

        for k in (0, 1, None):
            for d in (0, 1):
                if k is not None:
                    zb_got(d, 1, k)
                    yb(d, 1, k).start()
                    if k == 1:
                        zb(d, 2, None).start()
            if k == 0:
                for d in (0, 1):
                    for kk in (0, 1):
                        za_got(d, 1, 0, kk)
                    za(d, 2, 0, None).start()
                for d in (0, 1):
                    za_got(d, 1, 1, 0)
            elif k is None:
                for d in (0, 1):
                    za_got(d, 1, 1, 1)
                    za(d, 2, 1, None).start()
        for d in (0, 1):
            to_leaf(la_where(d, 1), r_la.at[d, 1]).start()
        y_done(0)
        for s in range(2, 5):
            for d in (0, 1):
                for k in (None,) if s < 4 else (0, 1):
                    zb_got(d, s, k)
                    if s < 3:
                        zb(d, s + 1, k).start()
                    elif s == 3:
                        zb(d, 4, 0).start()
                        zb(d, 4, 1).start()
                    yb(d, s, k).start()
            if s == 4:
                to_leaf(l4z_where(), r_lb.at[0, 4]).start()
                y_done(3)
                pl.semaphore_wait(ready, 1)
                for n in range(8):
                    send_or_keep(ids_out.at[0], ids_in.at[group], s_ids.at[0], r_ids, at(n // 2, n % 2, y, z))
                    send(ids_out.at[1], ids_in.at[group], s_ids.at[1], r_ids, at(n // 2, n % 2, across, z)).start()
                for n in range(7):
                    if n > 4:
                        choose_rows(n)
                    give_rows(n)
            for d in (0, 1):
                za_got(d, s, 0, None)
                if s < 4:
                    za(d, s + 1, 0, None).start()
            if s < 4:
                y_done(s - 1)
            if s == 3:
                for n in range(5):
                    choose_rows(n)
            for d in (0, 1):
                za_got(d, s, 1, None)
                if s < 4:
                    za(d, s + 1, 1, None).start()
            for d in dirs(s):
                to_leaf(la_where(d, s), r_la.at[d, s]).start()
        for d in (0, 1):
            yb_got(d, 4, 0)
            yb_got(d, 4, 1)
            to_leaf(l4y_where(d), r_l4.at[d]).start()
        choose_rows(7)
        give_rows(7)
        sent(e.at[:, :, pl.ds(0, 960)], s_ring)
        sent(e, s_l)

    @pl.when(jnp.logical_not(is_hub))
    def _():
        def ext(n):
            r = pl.ds(0, HEAD) if n == 0 else pl.ds(HEAD, ROWS - HEAD)
            return send(emb.at[r], e.at[z, slot(0, 0), r], s_ext.at[n], r_ext.at[n], at(x, q, across, z))

        def part(n, k, base=CENT):
            return pl.ds(pl.multiple_of(base + ((x + n) % NX) * QUART + k * PIECE, PIECE), PIECE)

        def cross(k):
            return send(cen.at[part(0, k, 0)], c.at[part(0, k)], s_c, r_cc.at[k], at(x, 1 - q, across, z))

        def near(d, k):
            to = at((x + 1 + 2 * d) % NX, q, y, z)
            return send(c.at[part(0, k)], c.at[part(0, k)], s_c, r_x1.at[d, k], to)

        def far(k):
            d = k // (PIECES // 2)
            to = at((x + 1 + 2 * d) % NX, q, y, z)
            which = part(3 - 2 * d, k)
            return send(c.at[which], c.at[which], s_c, r_x2.at[k], to)

        def pass_on(k):
            for d in (0, 1):
                got(c.at[part(3 - 2 * d, k)], r_x1.at[d, k])
            far(k).start()

        def arrived(s, n):
            d = n % 2 if s == 0 else (n + 1) % 2
            got(la_where(d, s), r_la.at[d, s])
            got(lb_where(d, s), r_lb.at[d, s])
            score(n, 0)

        ext(0).start()
        ext(1).start()
        for n in (0, 1):
            ext(n).wait_send()
        for k in range(PIECES):
            cross(k).start()
        own_c.wait()
        norms(0, NX, 0)
        for k in range(PIECES):
            got(c.at[part(0, k)], r_cc.at[k])
            for d in (0, 1):
                near(d, k).start()
            if k > 1:
                pass_on(k - 2)
            if k == 3:
                arrived(0, 0)
        arrived(1, 1)
        for k in range(PIECES - 2, PIECES):
            pass_on(k)
        arrived(1, 2)
        norms(x, 2, CENT)
        norms(x + 3, 1, CENT)
        arrived(2, 3)
        arrived(2, 4)
        for k in range(PIECES):
            got(c.at[part(2, k)], r_x2.at[k])
        pl.semaphore_signal(ready, inc=1, device_id=at(x, h, y, z), device_id_type=pl.DeviceIdType.MESH)
        norms(x + 2, 1, CENT)
        for n in range(5):
            score(n, 1)
        for n in (5, 6):
            arrived(3, n)
            score(n, 1)
        got(la_where(0, 4), r_la.at[0, 4])
        last_score(0)
        got(l4z_where(), r_lb.at[0, 4])
        for d in (0, 1):
            got(l4y_where(d), r_l4.at[d])
            last_score(d + 1)
        for k in (4, 3, 5, 2, 6, 1, 7, 0):
            for yy in (3 - other_y, across, other_y, y):
                to = at(x, h, yy, (z + k) % NZ)
                send(best, best_y.at[y % 2, z], s_by, r_by, to).start()
        sent(c.at[pl.ds(0, CENT)], s_c)

    own_slice.wait()
    own_prior.wait()
    pr = prior[...].astype(F32)
    got(ids_in, r_ids)
    k_of = lax.broadcasted_iota(jnp.int32, (CENT, 128), 0).astype(F32)
    hot = jnp.concatenate(
        [
            jnp.where(jnp.maximum(ids_in[2 * n, 0:1], ids_in[2 * n + 1, 0:1]) == k_of, 1.0, 0.0).astype(BF16)
            for n in range(4)
        ],
        axis=1,
    )
    counts = dot(jnp.ones((8, SLICE), BF16), hot, NT)
    den[...] = pr + counts[0:1]
    for k in range(4):
        f = slice(k * 128, (k + 1) * 128)
        num[f, :] = pr * cs[:, f].astype(F32).T
    got(rows, r_sel)
    for k in range(4):
        f = slice(k * 128, (k + 1) * 128)
        taken = jnp.concatenate([rows[n, k] for n in range(8)], axis=0)
        num[f, :] += dot(taken.T, hot, NT)

    @pl.when(jnp.logical_not(is_hub))
    def _():
        sent(e.at[0, 0, pl.ds(0, 512)], s_by)

    @pl.when(is_hub)
    def _():
        sent(ids_in.at[pl.ds(0, 7)], s_ids.at[0])
        sent(ids_in, s_ids.at[1])
        for t in (0, 1):
            sent(sel.at[t], s_sel.at[t])

    got(best_y, r_by)
    m = best_y[0, 0]
    for n in range(1, 2 * NZ):
        m = jnp.maximum(m, best_y[n // NZ, n % NZ])
    top[...] = m


def on_device(embeddings, centroids, assignment, prior_counts):
    dma = pltpu.SemaphoreType.DMA
    both = lambda *shape: [dma(shape), dma(shape)]
    vmem, hbm = pl.BlockSpec(memory_space=pltpu.VMEM), pl.BlockSpec(memory_space=pltpu.HBM)
    placed = (embeddings, centroids, assignment.reshape(8, 128), prior_counts.reshape(1, CENT))
    placed = [pltpu.with_memory_space_constraint(v, pltpu.HBM) for v in placed]
    top, num, den = pl.pallas_call(
        kernel,
        out_shape=[
            jax.ShapeDtypeStruct((8, 128), F32),
            jax.ShapeDtypeStruct((SLICE, CENT), F32),
            jax.ShapeDtypeStruct((1, CENT), F32),
        ],
        in_specs=[hbm, hbm, hbm, hbm],
        out_specs=[vmem, vmem, vmem],
        scratch_shapes=[
            pltpu.VMEM((NZ, 4, ROWS, WIDTH), BF16),
            pltpu.VMEM((2 * CENT, FEAT), BF16),
            pltpu.VMEM((2 * CENT, ROWS), F32),
            pltpu.VMEM((CENT, SLICE), BF16),
            pltpu.VMEM((2, 4, NZ, CAP, WIDTH), BF16),
            pltpu.VMEM((NZ, CAP, WIDTH), BF16),
            pltpu.VMEM((8, 4, CAP, WIDTH), BF16),
            pltpu.VMEM((2, 8, 128), F32),
            pltpu.VMEM((8, 8, 128), F32),
            pltpu.VMEM((8, 128), jnp.int32),
            pltpu.VMEM((1, CENT), jnp.int32),
            pltpu.VMEM((2 * CAP, ROWS), BF16),
            pltpu.VMEM((2 * CENT, 1), F32),
            pltpu.VMEM((8, 128), F32),
            pltpu.VMEM((2, NZ, 8, 128), F32),
            dma(()), dma((2, 4, 2, 2)), dma((2, 4, 2)), dma((2,)), dma((2, 5, 2)),
            *both(2),
            dma(()), dma((2, 5)), dma((2, 5)), dma((2,)),
            dma(()), dma((PIECES,)), dma((2, PIECES)), dma((PIECES,)),
            dma((2,)), dma(()),
            dma((2,)), dma(()),
            *both(),
            *both(), *both(), dma(()), pltpu.SemaphoreType.REGULAR,
        ],
        compiler_params=pltpu.CompilerParams(
            collective_id=0, has_side_effects=True, vmem_limit_bytes=40 * 2**20
        ),
        name="score_and_update",
    )(*placed)
    return top.reshape(ROWS), num / den


def solution(mesh):
    placed = (P("dp", "cent"), P("cent", None), P("dp"), P("cent"))
    return jax.shard_map(
        on_device, mesh=mesh, in_specs=placed, out_specs=(P("dp"), P("dp", "cent")), check_vma=False
    )
```

```python
import jax
import jax.numpy as jnp
from jax import lax
from jax.experimental import pallas as pl
from jax.experimental.pallas import tpu as pltpu
from jax.sharding import PartitionSpec as P

NX, NY, NZ = 4, 4, 8
ROWS = 1024
WIDTH = 128
CENT = 512
FEAT = 4096
CAP = 64
SLICE = 512
HEAD = 480
STAGES = 0, 384, 640, 1024
QUART = CENT // NX
PIECES = 4
PIECE = QUART // PIECES
SLOT_Y = (0, 3, 1, 2)
F32, BF16 = jnp.float32, jnp.bfloat16
NT = (((1,), (1,)), ((), ()))
NN = (((1,), (0,)), ((), ()))


def dot(a, b, dims):
    return lax.dot_general(a, b, dims, preferred_element_type=F32)


def kernel(
    emb, cen, asg_hbm, prior_hbm, top, num, den,
    e, c, acc, cs, sel, spare, rows, ids_out, ids_in, asg, prior, pick, hn, best, best_y,
    s_ring, r_za, r_zb, r_ya, r_yb, s_ext, r_ext, s_l, r_la, r_lb, r_l4,
    s_c, r_cc, r_x1, r_x2, s_sel, r_sel, s_ids, r_ids, s_by, r_by,
    l_own, l_c, l_cs, l_asg, l_prior, ready,
):
    dp, ce = lax.axis_index("dp"), lax.axis_index("cent")
    x, q, y, z = dp // 2, dp % 2, ce // NZ, ce % NZ
    h = y // 2
    pair = ((y + 1) // 2) % 2
    other_y, across = y + 1 - 2 * (y % 2), 3 - y
    group = 2 * x + h
    is_hub = q == h

    def at(x_, q_, y_, z_):
        return (2 * x_ + q_, NZ * y_ + z_)

    def send(src, dst, ss, rs, dev):
        return pltpu.make_async_remote_copy(
            src_ref=src, dst_ref=dst, send_sem=ss, recv_sem=rs,
            device_id=dev, device_id_type=pl.DeviceIdType.MESH,
        )

    def got(dst, rs):
        send(dst, dst, s_ring, rs, (dp, ce)).wait_recv()

    def sent(src, ss):
        send(src, src, ss, r_by, (dp, ce)).wait_send()

    def slot(b, k):
        p = pair if b == 0 else 1 - pair
        if k is None:
            return pl.ds(2 * p, 2)
        return 2 * p + (h if k == 0 else 1 - h)

    def zof(d, s):
        return (z + NZ - s) % NZ if d == 0 else (z + s) % NZ

    def zon(n):
        far = (n + 1) // 2
        return (z + NZ + far * (1 - 2 * (n % 2))) % NZ

    def dirs(s):
        return (0,) if s in (0, 4) else (0, 1)

    def za_rows(d, s):
        return pl.ds(0, HEAD) if s < 4 else pl.ds(d * (HEAD // 2), HEAD // 2)

    def zb_rows(d, s):
        n = ROWS - HEAD
        return pl.ds(HEAD, n) if s < 4 else pl.ds(HEAD + d * (n // 2), n // 2)

    def za(d, s, b, k):
        where = e.at[zof(d, s - 1), slot(b, k), za_rows(d, s)]
        src = emb.at[za_rows(d, s)] if (s, b, k) == (1, 0, 0) else where
        return send(src, where, s_ring, r_za.at[d, s - 1, b, k or 0], at(x, q, y, zof(1 - d, 1)))

    def za_got(d, s, b, k):
        got(e.at[zof(d, s), slot(b, k), za_rows(d, s)], r_za.at[d, s - 1, b, k or 0])

    def zb(d, s, k):
        where = e.at[zof(d, s - 1), slot(0, k), zb_rows(d, s)]
        src = emb.at[zb_rows(d, s)] if (s, k) == (1, 0) else where
        return send(src, where, s_ring, r_zb.at[d, s - 1, k or 0], at(x, q, y, zof(1 - d, 1)))

    def zb_got(d, s, k):
        got(e.at[zof(d, s), slot(0, k), zb_rows(d, s)], r_zb.at[d, s - 1, k or 0])

    def ya(k):
        where = e.at[z, slot(0, k), pl.ds(0, HEAD)]
        src = emb.at[pl.ds(0, HEAD)] if k == 0 else where
        return send(src, where, s_ring, r_ya.at[k], at(x, q, other_y, z))

    def ya_got(k):
        got(e.at[z, slot(1, k), pl.ds(0, HEAD)], r_ya.at[k])

    def yb(d, s, k):
        where = e.at[zof(d, s), slot(0, k), zb_rows(d, s)]
        src = emb.at[zb_rows(d, s)] if (s, k) == (0, 0) else where
        return send(src, where, s_ring, r_yb.at[d, s, k or 0], at(x, q, other_y, z))

    def yb_got(d, s, k):
        got(e.at[zof(d, s), slot(1, k), zb_rows(d, s)], r_yb.at[d, s, k or 0])

    def to_leaf(where, rs):
        return send(where, where, s_l, rs, at(x, 1 - q, y, z))

    def la_where(d, s):
        return e.at[zof(d, s), :, pl.ds(0, HEAD)]

    def lb_where(d, s):
        return e.at[zof(d, s), :, pl.ds(HEAD, ROWS - HEAD)]

    def l4z_where():
        return e.at[zof(0, 4), slot(0, None), pl.ds(HEAD, ROWS - HEAD)]

    def l4y_where(d):
        return e.at[zof(d, 4), slot(1, None), zb_rows(d, 4)]

    def send_or_keep(src, dst, ss, rs, to, spare=None):
        same = (to[0] == dp) & (to[1] == ce)

        @pl.when(jnp.logical_not(same))
        def _():
            send(src, dst, ss, rs, to).start()

        @pl.when(same)
        def _():
            pltpu.make_async_copy(src, dst, rs).start()
            if spare is not None:
                pltpu.make_async_copy(src, spare, ss).start()

    def choose(t, y_to):
        a = asg[...] - CENT * (NZ * y_to + z)
        mask = (a >= 0) & (a < CENT)
        m = jnp.where(mask, 1.0, 0.0).astype(F32)
        mb = m.astype(BF16)
        i0 = lax.broadcasted_iota(jnp.int32, (128, 128), 0)
        i1 = lax.broadcasted_iota(jnp.int32, (128, 128), 1)
        before = dot(mb, jnp.where(i0 < i1, 1.0, 0.0).astype(BF16), NN)
        total = dot(mb, jnp.ones((128, 128), BF16), NN)
        v = jnp.where(mask, a + 1, 0)
        high, low = (v // 32).astype(F32), (v % 32).astype(F32)
        first = lax.broadcasted_iota(jnp.int32, (8, 128), 0) == 0
        rank_of = lax.broadcasted_iota(jnp.int32, (128, 128), 0).astype(F32)
        off = (CAP * h).astype(F32)
        run = jnp.zeros((1, 128), F32)
        ids = jnp.zeros((8, 128), F32)
        for i in range(8):
            here = m[i : i + 1] > 0.5
            rank = before[i : i + 1] + run
            run = run + total[i : i + 1]
            one = jnp.where((rank == rank_of) & here, 1.0, 0.0).astype(BF16)
            pick[CAP * t : CAP * (t + 1), 128 * i : 128 * (i + 1)] = one[:CAP]
            put = jnp.where((rank + off == rank_of) & here, 1.0, 0.0).astype(BF16)
            vals = jnp.where(first, high[i : i + 1], low[i : i + 1]).astype(BF16)
            ids = ids + dot(vals, put, NT)
        ids_out[t] = jnp.broadcast_to(32.0 * ids[0:1] + ids[1:2] - 1.0, (8, 128))

    def norms(first, count, base):
        @pl.loop(0, count)
        def _(i):
            part = jnp.zeros((128, 128), F32)
            r = pl.ds(pl.multiple_of(base + (first + i) % NX * 128, 128), 128)
            for k in range(FEAT // 128):
                v = c[r, k * 128 : (k + 1) * 128].astype(F32)
                part = part + v * v
            hn[r, :] = 0.5 * jnp.sum(part, axis=1, keepdims=True)

    def choose_rows(n):
        zo = zon(n)
        for k in range(4):
            got_rows = dot(pick[...], e[zo, k], NN).astype(BF16)
            for t in (0, 1):
                sel[t, k, zo] = got_rows[CAP * t : CAP * (t + 1)]

    def give_rows(n):
        zo = zon(n)
        for k in range(4):
            for t in (0, 1):
                to = at(SLOT_Y[k], zo // 4, across if t else y, z)
                src, dst = sel.at[t, k, zo], rows.at[group, zo % 4]
                if t:
                    send(src, dst, s_sel.at[t], r_sel, to).start()
                else:
                    send_or_keep(src, dst, s_sel.at[t], r_sel, to, spare.at[n])

    def product(n, r, cr):
        zo = zon(n)
        left = jnp.concatenate(
            [c[cr, pl.ds(pl.multiple_of(yy * 1024 + zo * 128, 128), 128)] for yy in SLOT_Y], axis=1
        )
        return dot(left, jnp.concatenate([e[zo, k, r] for k in range(4)], axis=1), NT)

    def score(n, t):
        cr = slice(CENT * t, CENT * (t + 1))
        if n == 0:
            acc[cr] = product(0, slice(None), cr)
        else:
            acc[cr] += product(n, slice(None), cr)

    def last_score(stage):
        lo, hi = STAGES[stage : stage + 2]
        r = slice(lo, hi)
        m = jnp.max(acc[:, r] + product(NZ - 1, r, slice(None)) - hn[...], axis=0, keepdims=True)
        for i in range(lo // 128, hi // 128):
            best[i : i + 1, :] = m[:, 128 * i - lo : 128 * (i + 1) - lo]

    barrier = pltpu.get_barrier_semaphore()
    own_slice = pltpu.make_async_copy(cen.at[:, pl.ds(pl.multiple_of(dp * SLICE, SLICE), SLICE)], cs, l_cs)
    own_asg = pltpu.make_async_copy(asg_hbm, asg, l_asg)
    own_prior = pltpu.make_async_copy(prior_hbm, prior, l_prior)
    own = pltpu.make_async_copy(emb, e.at[z, slot(0, 0)], l_own)
    own_c = pltpu.make_async_copy(cen, c.at[pl.ds(0, CENT)], l_c)
    own_prior.start()
    own_slice.start()
    peers = [(dp, NZ * y + (z + 1) % NZ), (dp, NZ * y + (z + NZ - 1) % NZ), (dp, NZ * other_y + z)]
    peers += [at(x, 1 - q, y, z), at(x, 1 - q, across, z), (dp, NZ * across + z)]
    peers += [((dp + 2) % 8, ce), ((dp + 6) % 8, ce)]
    for to in peers:
        pl.semaphore_signal(barrier, inc=1, device_id=to, device_id_type=pl.DeviceIdType.MESH)

    @pl.when(is_hub)
    def _():
        own_asg.start()
        own.start()

    @pl.when(jnp.logical_not(is_hub))
    def _():
        own_c.start()

    pl.semaphore_wait(barrier, len(peers))

    @pl.when(is_hub)
    def _():
        for d in (0, 1):
            zb(d, 1, 0).start()
        for d in (0, 1):
            za(d, 1, 0, 0).start()
        ya(0).start()
        yb(0, 0, 0).start()
        got(e.at[z, slot(0, 1), pl.ds(0, HEAD)], r_ext.at[0])
        ya(1).start()
        for d in (0, 1):
            za(d, 1, 0, 1).start()
        ya_got(0)
        for d in (0, 1):
            za(d, 1, 1, 0).start()
        own_asg.wait()
        choose(0, y)
        got(e.at[z, slot(0, 1), pl.ds(HEAD, ROWS - HEAD)], r_ext.at[1])
        for d in (0, 1):
            zb(d, 1, 1).start()
        yb(0, 0, 1).start()
        ya_got(1)
        for d in (0, 1):
            za(d, 1, 1, 1).start()
        own.wait()
        to_leaf(la_where(0, 0), r_la.at[0, 0]).start()
        choose(1, across)

        def y_done(s):
            for d in dirs(s):
                for k in (0, 1) if s < 2 else (None,):
                    yb_got(d, s, k)
                to_leaf(lb_where(d, s), r_lb.at[d, s]).start()

        for k in (0, 1, None):
            for d in (0, 1):
                if k is not None:
                    zb_got(d, 1, k)
                    yb(d, 1, k).start()
                    if k == 1:
                        zb(d, 2, None).start()
            if k == 0:
                for d in (0, 1):
                    for kk in (0, 1):
                        za_got(d, 1, 0, kk)
                    za(d, 2, 0, None).start()
                for d in (0, 1):
                    za_got(d, 1, 1, 0)
            elif k is None:
                for d in (0, 1):
                    za_got(d, 1, 1, 1)
                    za(d, 2, 1, None).start()
        for d in (0, 1):
            to_leaf(la_where(d, 1), r_la.at[d, 1]).start()
        y_done(0)
        for s in range(2, 5):
            for d in (0, 1):
                for k in (None,) if s < 4 else (0, 1):
                    zb_got(d, s, k)
                    if s < 3:
                        zb(d, s + 1, k).start()
                    elif s == 3:
                        zb(d, 4, 0).start()
                        zb(d, 4, 1).start()
                    yb(d, s, k).start()
            if s == 4:
                to_leaf(l4z_where(), r_lb.at[0, 4]).start()
                y_done(3)
                pl.semaphore_wait(ready, 1)
                for n in range(8):
                    send_or_keep(ids_out.at[0], ids_in.at[group], s_ids.at[0], r_ids, at(n // 2, n % 2, y, z))
                    send(ids_out.at[1], ids_in.at[group], s_ids.at[1], r_ids, at(n // 2, n % 2, across, z)).start()
                for n in range(7):
                    if n > 4:
                        choose_rows(n)
                    give_rows(n)
            for d in (0, 1):
                za_got(d, s, 0, None)
                if s < 4:
                    za(d, s + 1, 0, None).start()
            if s < 4:
                y_done(s - 1)
            if s == 3:
                for n in range(5):
                    choose_rows(n)
            for d in (0, 1):
                za_got(d, s, 1, None)
                if s < 4:
                    za(d, s + 1, 1, None).start()
            for d in dirs(s):
                to_leaf(la_where(d, s), r_la.at[d, s]).start()
        for d in (0, 1):
            yb_got(d, 4, 0)
            yb_got(d, 4, 1)
            to_leaf(l4y_where(d), r_l4.at[d]).start()
        choose_rows(7)
        give_rows(7)
        sent(e.at[:, :, pl.ds(0, 960)], s_ring)
        sent(e, s_l)

    @pl.when(jnp.logical_not(is_hub))
    def _():
        def ext(n):
            r = pl.ds(0, HEAD) if n == 0 else pl.ds(HEAD, ROWS - HEAD)
            return send(emb.at[r], e.at[z, slot(0, 0), r], s_ext.at[n], r_ext.at[n], at(x, q, across, z))

        def part(n, k, base=CENT):
            return pl.ds(pl.multiple_of(base + ((x + n) % NX) * QUART + k * PIECE, PIECE), PIECE)

        def cross(k):
            return send(cen.at[part(0, k, 0)], c.at[part(0, k)], s_c, r_cc.at[k], at(x, 1 - q, across, z))

        def near(d, k):
            to = at((x + 1 + 2 * d) % NX, q, y, z)
            return send(c.at[part(0, k)], c.at[part(0, k)], s_c, r_x1.at[d, k], to)

        def far(k):
            d = k // (PIECES // 2)
            to = at((x + 1 + 2 * d) % NX, q, y, z)
            which = part(3 - 2 * d, k)
            return send(c.at[which], c.at[which], s_c, r_x2.at[k], to)

        def pass_on(k):
            for d in (0, 1):
                got(c.at[part(3 - 2 * d, k)], r_x1.at[d, k])
            far(k).start()

        def arrived(s, n):
            d = n % 2 if s == 0 else (n + 1) % 2
            got(la_where(d, s), r_la.at[d, s])
            got(lb_where(d, s), r_lb.at[d, s])
            score(n, 0)

        ext(0).start()
        ext(1).start()
        for n in (0, 1):
            ext(n).wait_send()
        for k in range(PIECES):
            cross(k).start()
        own_c.wait()
        norms(0, NX, 0)
        for k in range(PIECES):
            got(c.at[part(0, k)], r_cc.at[k])
            for d in (0, 1):
                near(d, k).start()
            if k > 1:
                pass_on(k - 2)
            if k == 3:
                arrived(0, 0)
        arrived(1, 1)
        for k in range(PIECES - 2, PIECES):
            pass_on(k)
        arrived(1, 2)
        norms(x, 2, CENT)
        norms(x + 3, 1, CENT)
        arrived(2, 3)
        arrived(2, 4)
        for k in range(PIECES):
            got(c.at[part(2, k)], r_x2.at[k])
        pl.semaphore_signal(ready, inc=1, device_id=at(x, h, y, z), device_id_type=pl.DeviceIdType.MESH)
        norms(x + 2, 1, CENT)
        for n in range(5):
            score(n, 1)
        for n in (5, 6):
            arrived(3, n)
            score(n, 1)
        got(la_where(0, 4), r_la.at[0, 4])
        last_score(0)
        got(l4z_where(), r_lb.at[0, 4])
        for d in (0, 1):
            got(l4y_where(d), r_l4.at[d])
            last_score(d + 1)
        for k in (4, 3, 5, 2, 6, 1, 7, 0):
            for yy in (3 - other_y, across, other_y, y):
                to = at(x, h, yy, (z + k) % NZ)
                send(best, best_y.at[y % 2, z], s_by, r_by, to).start()
        sent(c.at[pl.ds(0, CENT)], s_c)

    own_slice.wait()
    own_prior.wait()
    pr = prior[...].astype(F32)
    got(ids_in, r_ids)
    k_of = lax.broadcasted_iota(jnp.int32, (CENT, 128), 0).astype(F32)
    hot = jnp.concatenate(
        [
            jnp.where(jnp.maximum(ids_in[2 * n, 0:1], ids_in[2 * n + 1, 0:1]) == k_of, 1.0, 0.0).astype(BF16)
            for n in range(4)
        ],
        axis=1,
    )
    counts = dot(jnp.ones((8, SLICE), BF16), hot, NT)
    den[...] = pr + counts[0:1]
    for k in range(4):
        f = slice(k * 128, (k + 1) * 128)
        num[f, :] = pr * cs[:, f].astype(F32).T
    got(rows, r_sel)
    for k in range(4):
        f = slice(k * 128, (k + 1) * 128)
        taken = jnp.concatenate([rows[n, k] for n in range(8)], axis=0)
        num[f, :] += dot(taken.T, hot, NT)

    @pl.when(jnp.logical_not(is_hub))
    def _():
        sent(e.at[0, 0, pl.ds(0, 512)], s_by)

    @pl.when(is_hub)
    def _():
        sent(ids_in.at[pl.ds(0, 7)], s_ids.at[0])
        sent(ids_in, s_ids.at[1])
        for t in (0, 1):
            sent(sel.at[t], s_sel.at[t])

    got(best_y, r_by)
    m = best_y[0, 0]
    for n in range(1, 2 * NZ):
        m = jnp.maximum(m, best_y[n // NZ, n % NZ])
    top[...] = m


def on_device(embeddings, centroids, assignment, prior_counts):
    dma = pltpu.SemaphoreType.DMA
    both = lambda *shape: [dma(shape), dma(shape)]
    vmem, hbm = pl.BlockSpec(memory_space=pltpu.VMEM), pl.BlockSpec(memory_space=pltpu.HBM)
    placed = (embeddings, centroids, assignment.reshape(8, 128), prior_counts.reshape(1, CENT))
    placed = [pltpu.with_memory_space_constraint(v, pltpu.HBM) for v in placed]
    top, num, den = pl.pallas_call(
        kernel,
        out_shape=[
            jax.ShapeDtypeStruct((8, 128), F32),
            jax.ShapeDtypeStruct((SLICE, CENT), F32),
            jax.ShapeDtypeStruct((1, CENT), F32),
        ],
        in_specs=[hbm, hbm, hbm, hbm],
        out_specs=[vmem, vmem, vmem],
        scratch_shapes=[
            pltpu.VMEM((NZ, 4, ROWS, WIDTH), BF16),
            pltpu.VMEM((2 * CENT, FEAT), BF16),
            pltpu.VMEM((2 * CENT, ROWS), F32),
            pltpu.VMEM((CENT, SLICE), BF16),
            pltpu.VMEM((2, 4, NZ, CAP, WIDTH), BF16),
            pltpu.VMEM((NZ, CAP, WIDTH), BF16),
            pltpu.VMEM((8, 4, CAP, WIDTH), BF16),
            pltpu.VMEM((2, 8, 128), F32),
            pltpu.VMEM((8, 8, 128), F32),
            pltpu.VMEM((8, 128), jnp.int32),
            pltpu.VMEM((1, CENT), jnp.int32),
            pltpu.VMEM((2 * CAP, ROWS), BF16),
            pltpu.VMEM((2 * CENT, 1), F32),
            pltpu.VMEM((8, 128), F32),
            pltpu.VMEM((2, NZ, 8, 128), F32),
            dma(()), dma((2, 4, 2, 2)), dma((2, 4, 2)), dma((2,)), dma((2, 5, 2)),
            *both(2),
            dma(()), dma((2, 5)), dma((2, 5)), dma((2,)),
            dma(()), dma((PIECES,)), dma((2, PIECES)), dma((PIECES,)),
            dma((2,)), dma(()),
            dma((2,)), dma(()),
            *both(),
            *both(), *both(), dma(()), pltpu.SemaphoreType.REGULAR,
        ],
        compiler_params=pltpu.CompilerParams(
            collective_id=0, has_side_effects=True, vmem_limit_bytes=40 * 2**20
        ),
        name="score_and_update",
    )(*placed)
    return top.reshape(ROWS), num / den


def solution(mesh):
    placed = (P("dp", "cent"), P("cent", None), P("dp"), P("cent"))
    return jax.shard_map(
        on_device, mesh=mesh, in_specs=placed, out_specs=(P("dp"), P("dp", "cent")), check_vma=False
    )
```
